32 devices in a mesh: groups: 2 (over x), blk: 16 (over z, y, core).
Axes of the slice: x: 2, y: 2, z: 4, core: 2. Of those that a mesh axis runs over, the one named last changes fastest.
Arguments:
- cache: bfloat16 [128, 128, 8192], P(('groups', 'blk')), parts along dimension 0, may hold values from -0.0625 to 0.0625
- queries: bfloat16 [4096, 8192], P(('groups', 'blk')), parts along dimension 0, may hold values from -6 to 6
- plan: int32 [32, 10], P('groups'), parts along dimension 0, may hold values from 0 to 63, as said below
- pair_codes: int32 [32, 8, 8], P(('groups', 'blk')), parts along dimension 0, may hold values from 0 to 9, as said below
Outputs:
- scores: float32 [32, 8, 8, 128, 128], P(('groups', 'blk')), parts along dimension 0
The draws below stay inside these ranges and needn't reach their ends.
There are 2 independent parts, one for each index of `groups`. The reference program is written for one: setup_inputs(seed, part) draws one part's arguments, and reference() takes and returns one part's arrays. A program takes and returns all parts, laid end to end along the dimension named above; each array names one. Nothing has to cross between parts.
Inputs may be any that keep to these rules, and one draw needn't show every extreme that they name: plan[i, a] is a block held by scorer (i + a + 1) mod 16, that is, it lies in [((i + a + 1) mod 16) * 4, ((i + a + 1) mod 16 + 1) * 4). `pair_codes`: the 8 codes of one scorer and step are distinct.
All inputs are finite; a program needn't handle non-finite values.
Results may differ from the reference program's by a relative error of at most 0.0003.
Values may be sent and summed in bfloat16 or wider, within the bound.
No kernel may reach another device: no remote copies, remote signals or barrier semaphores. Data moves between devices by JAX's collectives and lax.ppermute only.
A program may use at most 256 MiB of HBM per device.

```python
import jax
import jax.numpy as jnp
from jax import lax

K = 8192
ROWS = 128
BLK_DEV = 4
QB_DEV = 1
SLOTS = 10
STEPS = 8
PAIRS = 8
SCORERS = 16
CACHED = 64
QROWS = 2048


def draw_plan(key, part):
    key = jax.random.fold_in(key, 11)
    local = jax.random.randint(key, (SCORERS, SLOTS), 0, BLK_DEV).astype(jnp.int32)
    local = local.at[SCORERS - 1, 0].set(0)
    local = local.at[SCORERS - 2, 0].set(BLK_DEV - 1)
    holder = (jnp.arange(SCORERS, dtype=jnp.int32)[:, None] + jnp.arange(SLOTS, dtype=jnp.int32)[None, :] + 1) % SCORERS
    return (holder * BLK_DEV + local).astype(jnp.int32)


def draw_pair_codes(key, part):
    key = jax.random.fold_in(key, 23)
    choices_all = SLOTS * QB_DEV
    noise = jax.random.randint(key, (SCORERS, STEPS, choices_all), 0, 2 ** 20)
    keyed = noise * 64 + jnp.arange(choices_all, dtype=jnp.int32)
    order = jnp.argsort(keyed, axis=-1)
    return order[:, :, :PAIRS].astype(jnp.int32)


def block_scale(rng, extent, pieces, low, high):
    factor_of = 1.0
    for dim, parts in pieces:
        heights = jax.random.uniform(jax.random.fold_in(jax.random.fold_in(rng, 6), dim), (parts,), jnp.float32, low / len(pieces), high / len(pieces))
        factor_of = factor_of * jnp.repeat(jnp.exp(heights), extent[dim] // parts).reshape((-1,) + (1,) * (len(extent) - 1 - dim))
    return factor_of


def scatter_about(stream_key, extent, deviation, bound, shards=(), held_as=jnp.bfloat16):
    level = block_scale(stream_key, extent, shards, -0.22, 0.18) if shards else 1.0
    array = jax.random.normal(stream_key, extent, jnp.float32) * deviation * level
    return jnp.minimum(jnp.maximum(array, -bound), bound).astype(held_as)


def setup_inputs(seed: int = 0, part: int = 0) -> dict:
    key_list = jax.random.split(jax.random.key(seed), 5)
    own_keys = jax.random.split(jax.random.fold_in(key_list[4], part), 5)
    cache = scatter_about(own_keys[0], (CACHED, ROWS, K), K ** -0.5, 0.0625, ((0, 16),))
    queries = scatter_about(own_keys[1], (QROWS, K), 1.0, 6.0, ((0, 16),))
    plan = draw_plan(jax.random.fold_in(jax.random.fold_in(key_list[4], part), 71), part)
    pair_codes = draw_pair_codes(jax.random.fold_in(jax.random.fold_in(key_list[4], part), 71), part)
    return {"cache": cache, "queries": queries, "plan": plan, "pair_codes": pair_codes}


def reference(cache, queries, plan, pair_codes):
    qblocks = queries.reshape(SCORERS, QB_DEV, ROWS, K)

    def one_scorer(index):
        fetched = jnp.take(cache, plan[index], axis=0)
        tiles = []
        for step in range(STEPS):
            shard = lax.dynamic_index_in_dim(qblocks, ((index - step) % SCORERS).astype(jnp.int32), 0, keepdims=False)
            codes = pair_codes[index, step]
            left = jnp.take(fetched, codes // QB_DEV, axis=0).astype(jnp.float32)
            right = jnp.take(shard, codes % QB_DEV, axis=0).astype(jnp.float32)
            tiles.append(jnp.einsum("pik,pjk->pij", left, right))
        return jnp.stack(tiles)

    return lax.map(one_scorer, jnp.arange(SCORERS, dtype=jnp.int32))
```

```python
import jax
import jax.numpy as jnp
from jax import lax
from jax.sharding import PartitionSpec as P


def shifted(x, axis, by):
    size = lax.axis_size(axis)
    return lax.ppermute(x, axis, [(i, (i + by) % size) for i in range(size)])


def per_device(cache, queries, plan, pair_codes):
    count = lax.axis_size("blk")
    myself = lax.axis_index("blk")
    local_blocks, rows, width = cache.shape
    slots = plan.shape[1]
    steps = pair_codes.shape[1]
    qcount = queries.shape[0] // rows

    everyone = lax.all_gather(queries, "blk", axis=0, tiled=True)
    product = lax.dot_general(
        cache.reshape(local_blocks * rows, width),
        everyone,
        (((1,), (1,)), ((), ())),
        preferred_element_type=jnp.float32,
    )
    product = product.reshape(local_blocks, rows, count, qcount, rows)

    received = []
    for slot in range(slots):
        distance = slot + 1
        served = (myself - distance) % count
        wanted = plan[served, slot] - myself * local_blocks
        block = lax.dynamic_index_in_dim(product, wanted, 0, keepdims=False)
        shards = (served - jnp.arange(steps)) % count
        tiles = jnp.take(block, shards, axis=1)
        tiles = tiles.transpose(1, 2, 0, 3)
        received.append(shifted(tiles, "blk", -distance))
    received = jnp.stack(received, axis=1)
    received = received.reshape(steps, slots * qcount, rows, rows)
    scores = jax.vmap(lambda tiles, codes: jnp.take(tiles, codes, axis=0))(received, pair_codes[0])
    return scores[None]


def solution(mesh):
    placed = (
        P(("groups", "blk"), None, None),
        P(("groups", "blk"), None),
        P("groups", None),
        P(("groups", "blk"), None, None),
    )
    return jax.shard_map(
        per_device,
        mesh=mesh,
        in_specs=placed,
        out_specs=P(("groups", "blk"), None, None, None, None),
        check_vma=False,
    )
```

```python
import functools
import math

import jax
import jax.numpy as jnp
from jax import lax
from jax.experimental import pallas as pl
from jax.experimental.pallas import tpu as pltpu
from jax.sharding import PartitionSpec as P

LANES = 128
TOP = 32760.0
OCTAVE = 64.0
FLOOR = 2.0**-110


def shifted(x, axis, by):
    size = lax.axis_size(axis)
    return lax.ppermute(x, axis, [(i, (i + by) % size) for i in range(size)])


def pack_kernel(chunk, pieces, count, steps, meta, product, *outs):
    rows = LANES
    part = LANES // pieces
    vectors = count // pieces
    depth = steps // pieces
    place = lax.broadcasted_iota(jnp.int32, (rows, LANES), 1) // part
    line = lax.broadcasted_iota(jnp.int32, (16, LANES), 0)
    for slot, out in enumerate(outs):
        first = pl.multiple_of(meta[0, slot] * rows, rows)
        scorer = meta[1, slot]
        mask = place <= lax.rem(scorer, pieces)
        scales = jnp.zeros((16, LANES), jnp.int32)
        for q in range(depth):
            high = lax.rem(scorer + count - pieces * q, count) // pieces
            low = lax.rem(high + vectors - 1, vectors)
            x = jnp.where(
                mask,
                product[pl.ds(first, rows), pl.ds(pl.multiple_of(high * LANES, LANES), LANES)],
                product[pl.ds(first, rows), pl.ds(pl.multiple_of(low * LANES, LANES), LANES)],
            )
            if chunk:
                x = pltpu.roll(x, chunk * part, 1)
            peak = jnp.max(jnp.abs(x), axis=0, keepdims=True)
            code = jnp.ceil(jnp.log2(jnp.maximum(peak, FLOOR)) * OCTAVE)
            x = x * (jnp.exp2(code * (-1.0 / OCTAVE)) * TOP)
            x = jnp.clip(jnp.round(x), -32767.0, 32767.0)
            out[q * rows : (q + 1) * rows, :] = x.astype(jnp.int32).astype(jnp.int16)
            scales = jnp.where(line == q, code.astype(jnp.int32), scales)
        out[depth * rows : depth * rows + 16, :] = scales.astype(jnp.int16)


def pack(product, meta, chunk, pieces, count, steps, slots):
    height = (steps // pieces) * LANES + 16
    whole = pl.BlockSpec(memory_space=pltpu.VMEM)
    return pl.pallas_call(
        functools.partial(pack_kernel, chunk, pieces, count, steps),
        out_shape=[jax.ShapeDtypeStruct((height, LANES), jnp.int16)] * slots,
        in_specs=[pl.BlockSpec(memory_space=pltpu.SMEM), whole],
        out_specs=[whole] * slots,
        compiler_params=pltpu.CompilerParams(vmem_limit_bytes=32 * 2**20),
        cost_estimate=pl.CostEstimate(
            flops=slots * height * LANES * 8, bytes_accessed=product.size * 4 + slots * height * LANES * 2, transcendentals=0
        ),
        name="pack",
    )(meta, product)


def unpack_kernel(pieces, slots, depth, where, codes, *refs):
    count = pieces * slots
    messages, out, stage, sems = refs[:count], refs[count], refs[count + 1], refs[count + 2]
    step = pl.program_id(0)
    rows = LANES
    part = LANES // pieces

    @pl.when(step == 0)
    def _():
        copies = []
        for r in range(pieces):
            for slot in range(slots):
                index = r * slots + slot
                copies.append(pltpu.make_async_copy(messages[index], stage.at[r, slot], sems.at[index]))
        for copy in copies:
            copy.start()
        for copy in copies:
            copy.wait()

    shard = where[0] + where[1] - step
    piece = step // pieces
    place = lax.broadcasted_iota(jnp.int32, (rows, LANES), 1) // part
    line = lax.broadcasted_iota(jnp.int32, (16, LANES), 0)
    masks = [place == lax.rem(r + shard, pieces) for r in range(1, pieces)]
    narrow = lax.broadcasted_iota(jnp.int32, (1, LANES), 1) // part
    for pair in range(out.shape[1]):
        slot = codes[step, pair]
        first = pl.multiple_of(piece * rows, rows)
        tile = scale = None
        for r in range(pieces):
            x = stage[r, slot, pl.ds(first, rows), :].astype(jnp.int32)
            s = stage[r, slot, depth * rows : depth * rows + 16, :].astype(jnp.int32)
            s = jnp.max(jnp.where(line == piece, s, -(2**15)), axis=0, keepdims=True)
            if r == 0:
                tile, scale = x, s
            else:
                tile = jnp.where(masks[r - 1], x, tile)
                scale = jnp.where(narrow == lax.rem(r + shard, pieces), s, scale)
        factor = jnp.exp2(scale.astype(jnp.float32) * (1.0 / OCTAVE)) * (1.0 / TOP)
        out[0, pair] = tile.astype(jnp.float32) * factor


def unpack(messages, where, codes, pieces, slots, steps):
    depth = steps // pieces
    pairs = codes.shape[1]
    height = depth * LANES + 16
    smem = pl.BlockSpec(memory_space=pltpu.SMEM)
    return pl.pallas_call(
        functools.partial(unpack_kernel, pieces, slots, depth),
        grid=(steps,),
        out_shape=jax.ShapeDtypeStruct((steps, pairs, LANES, LANES), jnp.float32),
        in_specs=[smem, smem] + [pl.BlockSpec(memory_space=pl.ANY)] * len(messages),
        out_specs=pl.BlockSpec((1, pairs, LANES, LANES), lambda step: (step, 0, 0, 0)),
        scratch_shapes=[
            pltpu.VMEM((pieces, slots, height, LANES), jnp.int16),
            pltpu.SemaphoreType.DMA((pieces * slots,)),
        ],
        compiler_params=pltpu.CompilerParams(vmem_limit_bytes=32 * 2**20),
        cost_estimate=pl.CostEstimate(
            flops=steps * pairs * LANES * LANES * 8, bytes_accessed=steps * pairs * LANES * LANES * 8, transcendentals=0
        ),
        name="unpack",
    )(where, codes, *messages)


def per_device(cache, queries, plan, pair_codes):
    count = lax.axis_size("blk")
    myself = lax.axis_index("blk")
    local_blocks, rows, width = cache.shape
    slots = plan.shape[1]
    steps = pair_codes.shape[1]
    pieces = math.gcd(4, math.gcd(steps, count))
    part = rows // pieces

    hops = jnp.arange(1, slots + 1, dtype=jnp.int32)
    served = (myself.astype(jnp.int32) - hops) % count
    wanted = plan[served, hops - 1] - myself.astype(jnp.int32) * local_blocks
    meta = jnp.stack([wanted, served])
    flat = cache.reshape(local_blocks * rows, width)

    messages = []
    for chunk in range(pieces):
        start = ((myself + chunk) % pieces) * part
        mine = lax.dynamic_slice_in_dim(queries, start, part, 0)
        everyone = lax.all_gather(mine, "blk", axis=0, tiled=True)
        product = lax.dot_general(flat, everyone, (((1,), (1,)), ((), ())), preferred_element_type=jnp.float32)
        packed = pack(product, meta, chunk, pieces, count, steps, slots)
        for slot in range(slots):
            messages.append(shifted(packed[slot], "blk", -(slot + 1)))
    where = jnp.stack([myself.astype(jnp.int32), jnp.int32(count)])
    return unpack(messages, where, pair_codes[0], pieces, slots, steps)[None]


def solution(mesh):
    placed = (
        P(("groups", "blk"), None, None),
        P(("groups", "blk"), None),
        P("groups", None),
        P(("groups", "blk"), None, None),
    )
    return jax.shard_map(
        per_device,
        mesh=mesh,
        in_specs=placed,
        out_specs=P(("groups", "blk"), None, None, None, None),
        check_vma=False,
    )
```

```python
import functools
import math

import jax
import jax.numpy as jnp
from jax import lax
from jax.experimental import pallas as pl
from jax.experimental.pallas import tpu as pltpu
from jax.sharding import PartitionSpec as P

LANES = 128
TOP = 32760.0
OCTAVE = 64.0
FLOOR = 2.0**-110


def shifted(x, axis, by):
    size = lax.axis_size(axis)
    return lax.ppermute(x, axis, [(i, (i + by) % size) for i in range(size)])


def pack_kernel(chunk, pieces, count, steps, meta, product, *outs):
    rows = LANES
    part = LANES // pieces
    vectors = count // pieces
    depth = steps // pieces
    place = lax.broadcasted_iota(jnp.int32, (rows, LANES), 1) // part
    line = lax.broadcasted_iota(jnp.int32, (16, LANES), 0)
    for slot, out in enumerate(outs):
        first = pl.multiple_of(meta[0, slot] * rows, rows)
        scorer = meta[1, slot]
        mask = place <= lax.rem(scorer, pieces)
        scales = jnp.zeros((16, LANES), jnp.int32)
        for q in range(depth):
            high = lax.rem(scorer + count - pieces * q, count) // pieces
            low = lax.rem(high + vectors - 1, vectors)
            x = jnp.where(
                mask,
                product[pl.ds(first, rows), pl.ds(pl.multiple_of(high * LANES, LANES), LANES)],
                product[pl.ds(first, rows), pl.ds(pl.multiple_of(low * LANES, LANES), LANES)],
            )
            if chunk:
                x = pltpu.roll(x, chunk * part, 1)
            peak = jnp.max(jnp.abs(x), axis=0, keepdims=True)
            code = jnp.ceil(jnp.log2(jnp.maximum(peak, FLOOR)) * OCTAVE)
            x = x * (jnp.exp2(code * (-1.0 / OCTAVE)) * TOP)
            x = jnp.clip(jnp.round(x), -32767.0, 32767.0)
            out[q * rows : (q + 1) * rows, :] = x.astype(jnp.int32).astype(jnp.int16)
            scales = jnp.where(line == q, code.astype(jnp.int32), scales)
        out[depth * rows : depth * rows + 16, :] = scales.astype(jnp.int16)


def pack(product, meta, chunk, pieces, count, steps, slots):
    height = (steps // pieces) * LANES + 16
    whole = pl.BlockSpec(memory_space=pltpu.VMEM)
    return pl.pallas_call(
        functools.partial(pack_kernel, chunk, pieces, count, steps),
        out_shape=[jax.ShapeDtypeStruct((height, LANES), jnp.int16)] * slots,
        in_specs=[pl.BlockSpec(memory_space=pltpu.SMEM), whole],
        out_specs=[whole] * slots,
        compiler_params=pltpu.CompilerParams(vmem_limit_bytes=32 * 2**20),
        cost_estimate=pl.CostEstimate(
            flops=slots * height * LANES * 8, bytes_accessed=product.size * 4 + slots * height * LANES * 2, transcendentals=0
        ),
        name="pack",
    )(meta, product)


def unpack_kernel(pieces, slots, depth, where, codes, *refs):
    count = pieces * slots
    messages, out, stage, sems = refs[:count], refs[count], refs[count + 1], refs[count + 2]
    step = pl.program_id(0)
    rows = LANES
    part = LANES // pieces

    @pl.when(step == 0)
    def _():
        copies = []
        for r in range(pieces):
            for slot in range(slots):
                index = r * slots + slot
                copies.append(pltpu.make_async_copy(messages[index], stage.at[r, slot], sems.at[index]))
        for copy in copies:
            copy.start()
        for copy in copies:
            copy.wait()

    shard = where[0] + where[1] - step
    piece = step // pieces
    place = lax.broadcasted_iota(jnp.int32, (rows, LANES), 1) // part
    line = lax.broadcasted_iota(jnp.int32, (16, LANES), 0)
    masks = [place == lax.rem(r + shard, pieces) for r in range(1, pieces)]
    narrow = lax.broadcasted_iota(jnp.int32, (1, LANES), 1) // part
    for pair in range(out.shape[1]):
        slot = codes[step, pair]
        first = pl.multiple_of(piece * rows, rows)
        tile = scale = None
        for r in range(pieces):
            x = stage[r, slot, pl.ds(first, rows), :].astype(jnp.int32)
            s = stage[r, slot, depth * rows : depth * rows + 16, :].astype(jnp.int32)
            s = jnp.max(jnp.where(line == piece, s, -(2**15)), axis=0, keepdims=True)
            if r == 0:
                tile, scale = x, s
            else:
                tile = jnp.where(masks[r - 1], x, tile)
                scale = jnp.where(narrow == lax.rem(r + shard, pieces), s, scale)
        factor = jnp.exp2(scale.astype(jnp.float32) * (1.0 / OCTAVE)) * (1.0 / TOP)
        out[0, pair] = tile.astype(jnp.float32) * factor


def unpack(messages, where, codes, pieces, slots, steps):
    depth = steps // pieces
    pairs = codes.shape[1]
    height = depth * LANES + 16
    smem = pl.BlockSpec(memory_space=pltpu.SMEM)
    return pl.pallas_call(
        functools.partial(unpack_kernel, pieces, slots, depth),
        grid=(steps,),
        out_shape=jax.ShapeDtypeStruct((steps, pairs, LANES, LANES), jnp.float32),
        in_specs=[smem, smem] + [pl.BlockSpec(memory_space=pl.ANY)] * len(messages),
        out_specs=pl.BlockSpec((1, pairs, LANES, LANES), lambda step: (step, 0, 0, 0)),
        scratch_shapes=[
            pltpu.VMEM((pieces, slots, height, LANES), jnp.int16),
            pltpu.SemaphoreType.DMA((pieces * slots,)),
        ],
        compiler_params=pltpu.CompilerParams(vmem_limit_bytes=32 * 2**20),
        cost_estimate=pl.CostEstimate(
            flops=steps * pairs * LANES * LANES * 8, bytes_accessed=steps * pairs * LANES * LANES * 8, transcendentals=0
        ),
        name="unpack",
    )(where, codes, *messages)


def per_device(cache, queries, plan, pair_codes):
    count = lax.axis_size("blk")
    myself = lax.axis_index("blk")
    local_blocks, rows, width = cache.shape
    slots = plan.shape[1]
    steps = pair_codes.shape[1]
    pieces = math.gcd(2, math.gcd(steps, count))
    part = rows // pieces

    hops = jnp.arange(1, slots + 1, dtype=jnp.int32)
    served = (myself.astype(jnp.int32) - hops) % count
    wanted = plan[served, hops - 1] - myself.astype(jnp.int32) * local_blocks
    meta = jnp.stack([wanted, served])
    flat = cache.reshape(local_blocks * rows, width)

    messages = []
    for chunk in range(pieces):
        start = ((myself + chunk) % pieces) * part
        mine = lax.dynamic_slice_in_dim(queries, start, part, 0)
        everyone = lax.all_gather(mine, "blk", axis=0, tiled=True)
        product = lax.dot_general(flat, everyone, (((1,), (1,)), ((), ())), preferred_element_type=jnp.float32)
        packed = pack(product, meta, chunk, pieces, count, steps, slots)
        for slot in range(slots):
            messages.append(shifted(packed[slot], "blk", -(slot + 1)))
    where = jnp.stack([myself.astype(jnp.int32), jnp.int32(count)])
    return unpack(messages, where, pair_codes[0], pieces, slots, steps)[None]


def solution(mesh):
    placed = (
        P(("groups", "blk"), None, None),
        P(("groups", "blk"), None),
        P("groups", None),
        P(("groups", "blk"), None, None),
    )
    return jax.shard_map(
        per_device,
        mesh=mesh,
        in_specs=placed,
        out_specs=P(("groups", "blk"), None, None, None, None),
        check_vma=False,
    )
```

```python
import functools

import jax
import jax.numpy as jnp
from jax import lax
from jax.experimental import pallas as pl
from jax.experimental.pallas import tpu as pltpu
from jax.sharding import PartitionSpec as P

LANES = 128
TOP = 32760.0
OCTAVE = 64.0
FLOOR = 2.0**-110
PHASES = 2
DEPTH = 1024


def shifted(x, axis, by):
    size = lax.axis_size(axis)
    return lax.ppermute(x, axis, [(i, (i + by) % size) for i in range(size)])


def pack_tile(x):
    peak = jnp.max(jnp.abs(x), axis=0, keepdims=True)
    code = jnp.ceil(jnp.log2(jnp.maximum(peak, FLOOR)) * OCTAVE)
    x = x * (jnp.exp2(code * (-1.0 / OCTAVE)) * TOP)
    x = jnp.clip(jnp.round(x), -32767.0, 32767.0)
    return x.astype(jnp.int32).astype(jnp.int16), code.astype(jnp.int32)


def score_kernel(phase, count, steps, meta, cache, queries, *refs):
    outs, total = refs[:-1], refs[-1]
    k = pl.program_id(0)
    rows = LANES
    fresh = lax.dot_general(
        cache[...],
        queries[...].reshape(-1, queries.shape[-1]),
        (((1,), (1,)), ((), ())),
        preferred_element_type=jnp.float32,
    )

    @pl.when(k == 0)
    def _():
        total[...] = fresh

    @pl.when(k > 0)
    def _():
        total[...] += fresh

    @pl.when(k == pl.num_programs(0) - 1)
    def _():
        depth = steps // PHASES
        line = lax.broadcasted_iota(jnp.int32, (16, LANES), 0)
        for slot, out in enumerate(outs):
            first = pl.multiple_of(meta[0, slot] * rows, rows)
            scorer = meta[1, slot]
            offset = lax.rem(scorer - phase + count, PHASES)
            scales = jnp.zeros((16, LANES), jnp.int32)
            for t in range(depth):
                shard = lax.rem(scorer - offset - PHASES * t + count, count)
                column = pl.multiple_of((shard // PHASES) * LANES, LANES)
                packed, code = pack_tile(total[pl.ds(first, rows), pl.ds(column, LANES)])
                out[t * rows : (t + 1) * rows, :] = packed
                scales = jnp.where(line == t, code, scales)
            out[depth * rows : depth * rows + 16, :] = scales.astype(jnp.int16)


def score(meta, flat, everyone, phase, count, steps, slots):
    height = (steps // PHASES) * LANES + 16
    group, _, rows, width = everyone.shape
    return pl.pallas_call(
        functools.partial(score_kernel, phase, count, steps),
        grid=(width // DEPTH,),
        out_shape=[jax.ShapeDtypeStruct((height, LANES), jnp.int16)] * slots,
        in_specs=[
            pl.BlockSpec(memory_space=pltpu.SMEM),
            pl.BlockSpec((flat.shape[0], DEPTH), lambda k: (0, k)),
            pl.BlockSpec((group, None, rows, DEPTH), lambda k: (0, phase, 0, k)),
        ],
        out_specs=[pl.BlockSpec((height, LANES), lambda k: (0, 0))] * slots,
        scratch_shapes=[pltpu.VMEM((flat.shape[0], group * rows), jnp.float32)],
        compiler_params=pltpu.CompilerParams(
            vmem_limit_bytes=48 * 2**20, dimension_semantics=("arbitrary",)
        ),
        cost_estimate=pl.CostEstimate(
            flops=2 * flat.size * group * rows,
            bytes_accessed=2 * (flat.size + group * rows * width + slots * height * LANES),
            transcendentals=0,
        ),
        name="score",
    )(meta, flat, everyone)


def unpack_kernel(slots, depth, where, codes, *refs):
    count = PHASES * slots
    messages, out, stage, sems = refs[:count], refs[count], refs[count + 1], refs[count + 2]
    step = pl.program_id(0)
    rows = LANES

    @pl.when(step == 0)
    def _():
        copies = [
            pltpu.make_async_copy(messages[index], stage.at[index], sems.at[index]) for index in range(count)
        ]
        for copy in copies:
            copy.start()
        for copy in copies:
            copy.wait()

    phase = lax.rem(where[0] + where[1] - step, PHASES)
    piece = step // PHASES
    first = pl.multiple_of(piece * rows, rows)
    line = lax.broadcasted_iota(jnp.int32, (16, LANES), 0)
    for pair in range(out.shape[1]):
        index = phase * slots + codes[step, pair]
        tile = stage[index, pl.ds(first, rows), :].astype(jnp.int32).astype(jnp.float32)
        scale = stage[index, depth * rows : depth * rows + 16, :].astype(jnp.int32)
        scale = jnp.max(jnp.where(line == piece, scale, -(2**15)), axis=0, keepdims=True)
        out[0, pair] = tile * (jnp.exp2(scale.astype(jnp.float32) * (1.0 / OCTAVE)) * (1.0 / TOP))


def unpack(messages, where, codes, slots, steps):
    depth = steps // PHASES
    pairs = codes.shape[1]
    height = depth * LANES + 16
    smem = pl.BlockSpec(memory_space=pltpu.SMEM)
    return pl.pallas_call(
        functools.partial(unpack_kernel, slots, depth),
        grid=(steps,),
        out_shape=jax.ShapeDtypeStruct((steps, pairs, LANES, LANES), jnp.float32),
        in_specs=[smem, smem] + [pl.BlockSpec(memory_space=pl.ANY)] * len(messages),
        out_specs=pl.BlockSpec((1, pairs, LANES, LANES), lambda step: (step, 0, 0, 0)),
        scratch_shapes=[
            pltpu.VMEM((PHASES * slots, height, LANES), jnp.int16),
            pltpu.SemaphoreType.DMA((PHASES * slots,)),
        ],
        compiler_params=pltpu.CompilerParams(
            vmem_limit_bytes=32 * 2**20, dimension_semantics=("arbitrary",)
        ),
        cost_estimate=pl.CostEstimate(
            flops=steps * pairs * LANES * LANES * 2, bytes_accessed=steps * pairs * LANES * LANES * 6, transcendentals=0
        ),
        name="unpack",
    )(where, codes, *messages)


def per_device(cache, queries, plan, pair_codes):
    count = lax.axis_size("blk")
    myself = lax.axis_index("blk").astype(jnp.int32)
    local_blocks, rows, width = cache.shape
    slots = plan.shape[1]
    steps = pair_codes.shape[1]

    hops = jnp.arange(1, slots + 1, dtype=jnp.int32)
    served = (myself - hops) % count
    wanted = plan[served, hops - 1] - myself * local_blocks
    meta = jnp.stack([wanted, served])
    flat = cache.reshape(local_blocks * rows, width)

    everyone = lax.all_gather(queries, "blk", axis=0, tiled=True)
    everyone = everyone.reshape(count // PHASES, PHASES, rows, width)
    messages = []
    for phase in range(PHASES):
        packed = score(meta, flat, everyone, phase, count, steps, slots)
        for slot in range(slots):
            messages.append(shifted(packed[slot], "blk", -(slot + 1)))
    where = jnp.stack([myself, jnp.int32(count)])
    return unpack(messages, where, pair_codes[0], slots, steps)[None]


def solution(mesh):
    placed = (
        P(("groups", "blk"), None, None),
        P(("groups", "blk"), None),
        P("groups", None),
        P(("groups", "blk"), None, None),
    )
    return jax.shard_map(
        per_device,
        mesh=mesh,
        in_specs=placed,
        out_specs=P(("groups", "blk"), None, None, None, None),
        check_vma=False,
    )
```

```python
import functools

import jax
import jax.numpy as jnp
from jax import lax
from jax.experimental import pallas as pl
from jax.experimental.pallas import tpu as pltpu
from jax.sharding import PartitionSpec as P

LANES = 128
TOP = 32760.0
OCTAVE = 64.0
FLOOR = 2.0**-110
DEPTH = 2048


def pack_tile(x):
    peak = jnp.max(jnp.abs(x), axis=0, keepdims=True)
    code = jnp.ceil(jnp.log2(jnp.maximum(peak, FLOOR)) * OCTAVE)
    x = x * (jnp.exp2(code * (-1.0 / OCTAVE)) * TOP)
    x = jnp.clip(jnp.round(x), -32767.0, 32767.0)
    return x.astype(jnp.int32).astype(jnp.int16), code.astype(jnp.int32)


def score_kernel(count, steps, meta, cache, queries, after, *refs):
    outs, total = refs[:-1], refs[-1]
    k = pl.program_id(0)
    rows = LANES
    fresh = lax.dot_general(
        cache[...], queries[...], (((1,), (1,)), ((), ())), preferred_element_type=jnp.float32
    )

    @pl.when(k == 0)
    def _():
        total[...] = fresh

    @pl.when(k > 0)
    def _():
        total[...] += fresh

    @pl.when(k == pl.num_programs(0) - 1)
    def _():
        depth = steps // 2
        side = meta[2, 0]
        line = lax.broadcasted_iota(jnp.int32, (16, LANES), 0)
        for slot, out in enumerate(outs):
            first = pl.multiple_of(meta[0, slot] * rows, rows)
            scorer = meta[1, slot]
            scales = jnp.zeros((16, LANES), jnp.int32)
            for t in range(depth):
                step = lax.rem(scorer + 4 - 2 * side - t % 2, 4) + 4 * (t // 2)
                shard = lax.rem(scorer - step + count, count)
                column = pl.multiple_of(((shard // 4) * 2 + t % 2) * LANES, LANES)
                packed, code = pack_tile(total[pl.ds(first, rows), pl.ds(column, LANES)])
                out[t * rows : (t + 1) * rows, :] = packed
                scales = jnp.where(line == t, code, scales)
            out[depth * rows : depth * rows + 16, :] = scales.astype(jnp.int16)


def score(meta, flat, gathered, after, count, steps, slots):
    height = (steps // 2) * LANES + 16
    columns, width = gathered.shape
    return pl.pallas_call(
        functools.partial(score_kernel, count, steps),
        grid=(width // DEPTH,),
        out_shape=[jax.ShapeDtypeStruct((height, LANES), jnp.int16)] * slots,
        in_specs=[
            pl.BlockSpec(memory_space=pltpu.SMEM),
            pl.BlockSpec((flat.shape[0], DEPTH), lambda k: (0, k)),
            pl.BlockSpec((columns, DEPTH), lambda k: (0, k)),
            pl.BlockSpec(memory_space=pl.ANY),
        ],
        out_specs=[pl.BlockSpec((height, LANES), lambda k: (0, 0))] * slots,
        scratch_shapes=[pltpu.VMEM((flat.shape[0], columns), jnp.float32)],
        compiler_params=pltpu.CompilerParams(
            vmem_limit_bytes=48 * 2**20, dimension_semantics=("arbitrary",)
        ),
        cost_estimate=pl.CostEstimate(
            flops=2 * flat.size * columns,
            bytes_accessed=2 * (flat.size + gathered.size + slots * height * LANES),
            transcendentals=0,
        ),
        name="score",
    )(meta, flat, gathered, after)


def unpack_kernel(slots, depth, where, codes, *refs):
    count = 3 * slots
    messages, out, stage, sems = refs[:count], refs[count], refs[count + 1], refs[count + 2]
    step = pl.program_id(0)
    rows = LANES

    @pl.when(step == 0)
    def _():
        copies = [
            pltpu.make_async_copy(messages[index], stage.at[index], sems.at[index]) for index in range(count)
        ]
        for copy in copies:
            copy.start()
        for copy in copies:
            copy.wait()

    me, devices = where[0], where[1]
    shard = me + devices - step
    piece = (step // 4) * 2 + lax.rem(shard, 2)
    first = pl.multiple_of(piece * rows, rows)
    line = lax.broadcasted_iota(jnp.int32, (16, LANES), 0)
    for pair in range(out.shape[1]):
        slot = codes[step, pair]
        holder = me + 1 + slot
        same = lax.rem(holder // 2, 2) == lax.rem(shard // 2, 2)
        index = slot + jnp.where(same, 0, slots + slots * lax.rem(holder, 2))
        tile = stage[index, pl.ds(first, rows), :].astype(jnp.int32).astype(jnp.float32)
        scale = stage[index, depth * rows : depth * rows + 16, :].astype(jnp.int32)
        scale = jnp.max(jnp.where(line == piece, scale, -(2**15)), axis=0, keepdims=True)
        out[0, pair] = tile * (jnp.exp2(scale.astype(jnp.float32) * (1.0 / OCTAVE)) * (1.0 / TOP))


def unpack(messages, where, codes, slots, steps):
    depth = steps // 2
    pairs = codes.shape[1]
    height = depth * LANES + 16
    smem = pl.BlockSpec(memory_space=pltpu.SMEM)
    return pl.pallas_call(
        functools.partial(unpack_kernel, slots, depth),
        grid=(steps,),
        out_shape=jax.ShapeDtypeStruct((steps, pairs, LANES, LANES), jnp.float32),
        in_specs=[smem, smem] + [pl.BlockSpec(memory_space=pl.ANY)] * len(messages),
        out_specs=pl.BlockSpec((1, pairs, LANES, LANES), lambda step: (step, 0, 0, 0)),
        scratch_shapes=[
            pltpu.VMEM((len(messages), height, LANES), jnp.int16),
            pltpu.SemaphoreType.DMA((len(messages),)),
        ],
        compiler_params=pltpu.CompilerParams(
            vmem_limit_bytes=32 * 2**20, dimension_semantics=("arbitrary",)
        ),
        cost_estimate=pl.CostEstimate(
            flops=steps * pairs * LANES * LANES * 2, bytes_accessed=steps * pairs * LANES * LANES * 6, transcendentals=0
        ),
        name="unpack",
    )(where, codes, *messages)


def returns(packed, pairs_of):
    slots = len(packed)
    received = [None] * slots
    for slot in reversed(range(slots)):
        received[slot] = lax.ppermute(packed[slot], "blk", pairs_of(slot))
    return received


def per_device(cache, queries, plan, pair_codes):
    count = lax.axis_size("blk")
    myself = lax.axis_index("blk").astype(jnp.int32)
    local_blocks, rows, width = cache.shape
    slots = plan.shape[1]
    steps = pair_codes.shape[1]
    side = (myself // 2) % 2
    partner = myself + 2 - 4 * side

    hops = jnp.arange(1, slots + 1, dtype=jnp.int32)

    def meta_of(holder):
        served = (holder - hops) % count
        wanted = plan[served, hops - 1] - holder * local_blocks
        return jnp.stack([wanted, served, jnp.broadcast_to(side, served.shape)])

    flat = cache.reshape(local_blocks * rows, width)
    sides = [[d for d in range(count) if (d // 2) % 2 == y] for y in range(2)]
    gathered = lax.all_gather(queries, "blk", axis=0, tiled=True, axis_index_groups=sides)

    early = lax.ppermute(flat, "blk", [(d, d ^ 2) for d in range(0, count, 2)])
    token = lax.ppermute(early[:16, :LANES], "blk", [(d, d ^ 1) for d in range(count)])
    flat_late, token = lax.optimization_barrier((flat, token))
    late = lax.ppermute(flat_late, "blk", [(d, d ^ 2) for d in range(1, count, 2)])

    own = score(meta_of(myself), flat, gathered, plan, count, steps, slots)
    messages = returns(own, lambda slot: [(d, (d - slot - 1) % count) for d in range(count)])
    for parity, blocks in enumerate((early, late)):
        packed = score(meta_of(partner), blocks, gathered, token, count, steps, slots)
        messages += returns(
            packed, lambda slot: [(d, ((d ^ 2) - slot - 1) % count) for d in range(parity, count, 2)]
        )
    where = jnp.stack([myself, jnp.int32(count)])
    return unpack(messages, where, pair_codes[0], slots, steps)[None]


def solution(mesh):
    placed = (
        P(("groups", "blk"), None, None),
        P(("groups", "blk"), None),
        P("groups", None),
        P(("groups", "blk"), None, None),
    )
    return jax.shard_map(
        per_device,
        mesh=mesh,
        in_specs=placed,
        out_specs=P(("groups", "blk"), None, None, None, None),
        check_vma=False,
    )
```

```python
import functools

import jax
import jax.numpy as jnp
from jax import lax
from jax.experimental import pallas as pl
from jax.experimental.pallas import tpu as pltpu
from jax.sharding import PartitionSpec as P

LANES = 128
TOP = 32760.0
OCTAVE = 64.0
FLOOR = 2.0**-110
PHASES = 2
DEPTH = 2048


def shifted(x, axis, by):
    size = lax.axis_size(axis)
    return lax.ppermute(x, axis, [(i, (i + by) % size) for i in range(size)])


def pack_tile(x):
    peak = jnp.max(jnp.abs(x), axis=0, keepdims=True)
    code = jnp.ceil(jnp.log2(jnp.maximum(peak, FLOOR)) * OCTAVE)
    x = x * (jnp.exp2(code * (-1.0 / OCTAVE)) * TOP)
    x = jnp.clip(jnp.round(x), -32767.0, 32767.0)
    return x.astype(jnp.int32).astype(jnp.int16), code.astype(jnp.int32)


def score_kernel(phase, count, steps, order, meta, cache, queries, *refs):
    outs, total = refs[:-1], refs[-1]
    k = pl.program_id(0)
    rows = LANES
    fresh = lax.dot_general(
        cache[...],
        queries[...].reshape(-1, queries.shape[-1]),
        (((1,), (1,)), ((), ())),
        preferred_element_type=jnp.float32,
    )

    @pl.when(k == 0)
    def _():
        total[...] = fresh

    @pl.when(k > 0)
    def _():
        total[...] += fresh

    @pl.when(k == pl.num_programs(0) - 1)
    def _():
        depth = steps // PHASES
        line = lax.broadcasted_iota(jnp.int32, (16, LANES), 0)
        for slot, out in zip(order, outs):
            first = pl.multiple_of(meta[0, slot] * rows, rows)
            scorer = meta[1, slot]
            offset = lax.rem(scorer - phase + count, PHASES)
            scales = jnp.zeros((16, LANES), jnp.int32)
            for t in range(depth):
                shard = lax.rem(scorer - offset - PHASES * t + count, count)
                column = pl.multiple_of((shard // PHASES) * LANES, LANES)
                packed, code = pack_tile(total[pl.ds(first, rows), pl.ds(column, LANES)])
                out[t * rows : (t + 1) * rows, :] = packed
                scales = jnp.where(line == t, code, scales)
            out[depth * rows : depth * rows + 16, :] = scales.astype(jnp.int16)


def score(meta, flat, everyone, phase, count, steps, order):
    slots = len(order)
    height = (steps // PHASES) * LANES + 16
    group, _, rows, width = everyone.shape
    return pl.pallas_call(
        functools.partial(score_kernel, phase, count, steps, order),
        grid=(width // DEPTH,),
        out_shape=[jax.ShapeDtypeStruct((height, LANES), jnp.int16)] * slots,
        in_specs=[
            pl.BlockSpec(memory_space=pltpu.SMEM),
            pl.BlockSpec((flat.shape[0], DEPTH), lambda k: (0, k)),
            pl.BlockSpec((group, None, rows, DEPTH), lambda k: (0, phase, 0, k)),
        ],
        out_specs=[pl.BlockSpec((height, LANES), lambda k: (0, 0))] * slots,
        scratch_shapes=[pltpu.VMEM((flat.shape[0], group * rows), jnp.float32)],
        compiler_params=pltpu.CompilerParams(
            vmem_limit_bytes=48 * 2**20, dimension_semantics=("arbitrary",)
        ),
        cost_estimate=pl.CostEstimate(
            flops=2 * flat.size * group * rows,
            bytes_accessed=2 * (flat.size + group * rows * width + slots * height * LANES),
            transcendentals=0,
        ),
        name="score",
    )(meta, flat, everyone)


def unpack_kernel(order, depth, where, codes, *refs):
    out, stage, sems = refs[-3:]
    turn = pl.program_id(0)
    rows = LANES

    @pl.when(turn == 0)
    def _():
        copies = [
            pltpu.make_async_copy(message, stage.at[slot], sems.at[slot]) for slot, message in zip(order, refs)
        ]
        for copy in copies:
            copy.start()
        for copy in copies:
            copy.wait()

    step = PHASES * turn + where[0]
    first = pl.multiple_of(turn * rows, rows)
    line = lax.broadcasted_iota(jnp.int32, (16, LANES), 0)
    for pair in range(out.shape[1]):
        slot = codes[step, pair]
        tile = stage[slot, pl.ds(first, rows), :].astype(jnp.int32).astype(jnp.float32)
        scale = stage[slot, depth * rows : depth * rows + 16, :].astype(jnp.int32)
        scale = jnp.max(jnp.where(line == turn, scale, -(2**15)), axis=0, keepdims=True)
        out[0, pair] = tile * (jnp.exp2(scale.astype(jnp.float32) * (1.0 / OCTAVE)) * (1.0 / TOP))


def unpack(messages, where, codes, order, steps, before=None):
    slots = len(order)
    depth = steps // PHASES
    pairs = codes.shape[1]
    height = depth * LANES + 16
    operands = [where, codes, *messages] + ([] if before is None else [before])
    return pl.pallas_call(
        functools.partial(unpack_kernel, order, depth),
        out_shape=jax.ShapeDtypeStruct((steps, pairs, LANES, LANES), jnp.float32),
        grid_spec=pltpu.PrefetchScalarGridSpec(
            num_scalar_prefetch=2,
            grid=(depth,),
            in_specs=[pl.BlockSpec(memory_space=pl.ANY)] * (len(operands) - 2),
            out_specs=pl.BlockSpec(
                (1, pairs, LANES, LANES), lambda turn, where, codes: (PHASES * turn + where[0], 0, 0, 0)
            ),
            scratch_shapes=[
                pltpu.VMEM((slots, height, LANES), jnp.int16),
                pltpu.SemaphoreType.DMA((slots,)),
            ],
        ),
        input_output_aliases={} if before is None else {len(operands) - 1: 0},
        compiler_params=pltpu.CompilerParams(
            vmem_limit_bytes=32 * 2**20, dimension_semantics=("arbitrary",)
        ),
        cost_estimate=pl.CostEstimate(
            flops=depth * pairs * LANES * LANES * 2, bytes_accessed=depth * pairs * LANES * LANES * 6, transcendentals=0
        ),
        name="unpack",
    )(*operands)


def per_device(cache, queries, plan, pair_codes):
    count = lax.axis_size("blk")
    myself = lax.axis_index("blk").astype(jnp.int32)
    local_blocks, rows, width = cache.shape
    slots = plan.shape[1]
    steps = pair_codes.shape[1]

    hops = jnp.arange(1, slots + 1, dtype=jnp.int32)
    served = (myself - hops) % count
    wanted = plan[served, hops - 1] - myself * local_blocks
    meta = jnp.stack([wanted, served])
    flat = cache.reshape(local_blocks * rows, width)

    everyone = lax.all_gather(queries, "blk", axis=0, tiled=True)
    everyone = everyone.reshape(count // PHASES, PHASES, rows, width)
    order = [slot for pair in zip(reversed(range(slots)), range(slots)) for slot in pair][:slots]
    assert sorted(order) == list(range(slots))
    received = []
    for phase in range(PHASES):
        packed = score(meta, flat, everyone, phase, count, steps, order)
        received.append([shifted(tiles, "blk", -(slot + 1)) for slot, tiles in zip(order, packed)])
    scores = None
    for phase in range(PHASES):
        where = ((myself + phase) % PHASES).reshape(1)
        scores = unpack(received[phase], where, pair_codes[0], order, steps, scores)
    return scores[None]


def solution(mesh):
    placed = (
        P(("groups", "blk"), None, None),
        P(("groups", "blk"), None),
        P("groups", None),
        P(("groups", "blk"), None, None),
    )
    return jax.shard_map(
        per_device,
        mesh=mesh,
        in_specs=placed,
        out_specs=P(("groups", "blk"), None, None, None, None),
        check_vma=False,
    )
```

```python
import functools

import jax
import jax.numpy as jnp
from jax import lax
from jax.experimental import pallas as pl
from jax.experimental.pallas import tpu as pltpu
from jax.sharding import PartitionSpec as P

LANES = 128
TOP = 32760.0
OCTAVE = 64.0
FLOOR = 2.0**-110
PHASES = ((6, 2), (0, 3), (3, 3))
DEPTH = 2048


def shifted(x, axis, by):
    size = lax.axis_size(axis)
    return lax.ppermute(x, axis, [(i, (i + by) % size) for i in range(size)])


def pack_tile(x):
    peak = jnp.max(jnp.abs(x), axis=0, keepdims=True)
    code = jnp.ceil(jnp.log2(jnp.maximum(peak, FLOOR)) * OCTAVE)
    x = x * (jnp.exp2(code * (-1.0 / OCTAVE)) * TOP)
    x = jnp.clip(jnp.round(x), -32767.0, 32767.0)
    return x.astype(jnp.int32).astype(jnp.int16), code.astype(jnp.int32)


def score_kernel(phase, count, steps, order, meta, cache, queries, *refs):
    outs, total = refs[:-1], refs[-1]
    k = pl.program_id(0)
    rows = LANES
    fresh = lax.dot_general(
        cache[...],
        queries[...].reshape(-1, queries.shape[-1]),
        (((1,), (1,)), ((), ())),
        preferred_element_type=jnp.float32,
    )

    @pl.when(k == 0)
    def _():
        total[...] = fresh

    @pl.when(k > 0)
    def _():
        total[...] += fresh

    @pl.when(k == pl.num_programs(0) - 1)
    def _():
        start, depth = phase
        line = lax.broadcasted_iota(jnp.int32, (16, LANES), 0)
        for slot, out in zip(order, outs):
            first = pl.multiple_of(meta[0, slot] * rows, rows)
            scorer = meta[1, slot]
            scales = jnp.zeros((16, LANES), jnp.int32)
            for t in range(depth):
                step = lax.rem(scorer - start - t + count, steps)
                shard = lax.rem(scorer - step + count, count)
                column = pl.multiple_of(((shard // steps) * depth + t) * LANES, LANES)
                packed, code = pack_tile(total[pl.ds(first, rows), pl.ds(column, LANES)])
                out[t * rows : (t + 1) * rows, :] = packed
                scales = jnp.where(line == t, code, scales)
            out[depth * rows : depth * rows + 16, :] = scales.astype(jnp.int16)


def score(meta, flat, everyone, phase, count, steps, order):
    slots = len(order)
    start, depth = phase
    height = depth * LANES + 16
    group, _, rows, width = everyone.shape
    columns = group * depth * rows
    return pl.pallas_call(
        functools.partial(score_kernel, phase, count, steps, order),
        grid=(width // DEPTH,),
        out_shape=[jax.ShapeDtypeStruct((height, LANES), jnp.int16)] * slots,
        in_specs=[
            pl.BlockSpec(memory_space=pltpu.SMEM),
            pl.BlockSpec((flat.shape[0], DEPTH), lambda k: (0, k)),
            pl.BlockSpec((group, depth, rows, DEPTH), lambda k: (0, start // depth, 0, k)),
        ],
        out_specs=[pl.BlockSpec((height, LANES), lambda k: (0, 0))] * slots,
        scratch_shapes=[pltpu.VMEM((flat.shape[0], columns), jnp.float32)],
        compiler_params=pltpu.CompilerParams(
            vmem_limit_bytes=48 * 2**20, dimension_semantics=("arbitrary",)
        ),
        cost_estimate=pl.CostEstimate(
            flops=2 * flat.size * columns,
            bytes_accessed=2 * (flat.size + columns * width + slots * height * LANES),
            transcendentals=0,
        ),
        name="score",
    )(meta, flat, everyone)


def unpack_kernel(order, depth, steps, where, codes, *refs):
    out, stage, sems = refs[-3:]
    turn = pl.program_id(0)
    rows = LANES

    @pl.when(turn == 0)
    def _():
        copies = [
            pltpu.make_async_copy(message, stage.at[slot], sems.at[slot]) for slot, message in zip(order, refs)
        ]
        for copy in copies:
            copy.start()
        for copy in copies:
            copy.wait()

    step = lax.rem(where[0] - turn + steps, steps)
    first = pl.multiple_of(turn * rows, rows)
    line = lax.broadcasted_iota(jnp.int32, (16, LANES), 0)
    for pair in range(out.shape[1]):
        slot = codes[step, pair]
        tile = stage[slot, pl.ds(first, rows), :].astype(jnp.int32).astype(jnp.float32)
        scale = stage[slot, depth * rows : depth * rows + 16, :].astype(jnp.int32)
        scale = jnp.max(jnp.where(line == turn, scale, -(2**15)), axis=0, keepdims=True)
        out[0, pair] = tile * (jnp.exp2(scale.astype(jnp.float32) * (1.0 / OCTAVE)) * (1.0 / TOP))


def unpack(messages, where, codes, depth, order, steps, before=None):
    slots = len(order)
    pairs = codes.shape[1]
    height = depth * LANES + 16
    operands = [where, codes, *messages] + ([] if before is None else [before])
    return pl.pallas_call(
        functools.partial(unpack_kernel, order, depth, steps),
        out_shape=jax.ShapeDtypeStruct((steps, pairs, LANES, LANES), jnp.float32),
        grid_spec=pltpu.PrefetchScalarGridSpec(
            num_scalar_prefetch=2,
            grid=(depth,),
            in_specs=[pl.BlockSpec(memory_space=pl.ANY)] * (len(operands) - 2),
            out_specs=pl.BlockSpec(
                (1, pairs, LANES, LANES),
                lambda turn, where, codes: (lax.rem(where[0] - turn + steps, steps), 0, 0, 0),
            ),
            scratch_shapes=[
                pltpu.VMEM((slots, height, LANES), jnp.int16),
                pltpu.SemaphoreType.DMA((slots,)),
            ],
        ),
        input_output_aliases={} if before is None else {len(operands) - 1: 0},
        compiler_params=pltpu.CompilerParams(
            vmem_limit_bytes=32 * 2**20, dimension_semantics=("arbitrary",)
        ),
        cost_estimate=pl.CostEstimate(
            flops=depth * pairs * LANES * LANES * 2, bytes_accessed=depth * pairs * LANES * LANES * 6, transcendentals=0
        ),
        name="unpack",
    )(*operands)


def per_device(cache, queries, plan, pair_codes):
    count = lax.axis_size("blk")
    myself = lax.axis_index("blk").astype(jnp.int32)
    local_blocks, rows, width = cache.shape
    slots = plan.shape[1]
    steps = pair_codes.shape[1]

    hops = jnp.arange(1, slots + 1, dtype=jnp.int32)
    served = (myself - hops) % count
    wanted = plan[served, hops - 1] - myself * local_blocks
    meta = jnp.stack([wanted, served])
    flat = cache.reshape(local_blocks * rows, width)

    everyone = lax.all_gather(queries, "blk", axis=0, tiled=True)
    everyone = everyone.reshape(count // steps, steps, rows, width)
    order = [slot for pair in zip(reversed(range(slots)), range(slots)) for slot in pair][:slots]
    assert sorted(order) == list(range(slots)) and sum(depth for _, depth in PHASES) == steps
    received = []
    for phase in PHASES:
        packed = score(meta, flat, everyone, phase, count, steps, order)
        received.append([shifted(tiles, "blk", -(slot + 1)) for slot, tiles in zip(order, packed)])
    scores = None
    for (start, depth), messages in zip(PHASES, received):
        where = ((myself - start) % steps).reshape(1)
        scores = unpack(messages, where, pair_codes[0], depth, order, steps, scores)
    return scores[None]


def solution(mesh):
    placed = (
        P(("groups", "blk"), None, None),
        P(("groups", "blk"), None),
        P("groups", None),
        P(("groups", "blk"), None, None),
    )
    return jax.shard_map(
        per_device,
        mesh=mesh,
        in_specs=placed,
        out_specs=P(("groups", "blk"), None, None, None, None),
        check_vma=False,
    )
```

```python
import functools

import jax
import jax.numpy as jnp
from jax import lax
from jax.experimental import pallas as pl
from jax.experimental.pallas import tpu as pltpu
from jax.sharding import PartitionSpec as P

LANES = 128
TOP = 32760.0
OCTAVE = 64.0
FLOOR = 2.0**-110
DEPTH = 2048
PARTS = 4


def pack_tile(x):
    peak = jnp.max(jnp.abs(x), axis=0, keepdims=True)
    code = jnp.ceil(jnp.log2(jnp.maximum(peak, FLOOR)) * OCTAVE)
    x = x * (jnp.exp2(code * (-1.0 / OCTAVE)) * TOP)
    x = jnp.clip(jnp.round(x), -32767.0, 32767.0)
    return x.astype(jnp.int32).astype(jnp.int16), code.astype(jnp.int32)


def multiply(cache, pieces):
    rows = jnp.concatenate([piece[...] for piece in pieces], axis=0)
    return lax.dot_general(cache[...], rows, (((1,), (1,)), ((), ())), preferred_element_type=jnp.float32)


def early_kernel(cache, *refs):
    pieces, out = refs[:-1], refs[-1]
    fresh = multiply(cache, pieces)

    @pl.when(pl.program_id(0) == 0)
    def _():
        out[...] = fresh

    @pl.when(pl.program_id(0) > 0)
    def _():
        out[...] += fresh


def piece_spec(piece):
    return pl.BlockSpec((piece.shape[0], DEPTH), lambda k: (0, k))


def early(flat, pieces):
    columns = sum(piece.shape[0] for piece in pieces)
    height, width = flat.shape
    return pl.pallas_call(
        early_kernel,
        grid=(width // DEPTH,),
        out_shape=jax.ShapeDtypeStruct((height, columns), jnp.float32),
        in_specs=[piece_spec(flat)] + [piece_spec(piece) for piece in pieces],
        out_specs=pl.BlockSpec((height, columns), lambda k: (0, 0)),
        compiler_params=pltpu.CompilerParams(
            vmem_limit_bytes=48 * 2**20, dimension_semantics=("arbitrary",)
        ),
        cost_estimate=pl.CostEstimate(
            flops=2 * flat.size * columns, bytes_accessed=2 * (height + columns) * width, transcendentals=0
        ),
        name="early",
    )(flat, *pieces)


def score_kernel(count, order, depth, meta, cache, done, *refs):
    pieces, outs, total = refs[:count], refs[count:-1], refs[-1]
    k = pl.program_id(0)
    rows = LANES
    have = done.shape[1]
    fresh = multiply(cache, pieces)

    @pl.when(k == 0)
    def _():
        total[:, :have] = done[...]
        total[:, have:] = fresh

    @pl.when(k > 0)
    def _():
        total[:, have:] += fresh

    @pl.when(k == pl.num_programs(0) - 1)
    def _():
        line = lax.broadcasted_iota(jnp.int32, (16, LANES), 0)
        for slot, out in zip(order, outs):
            first = pl.multiple_of(meta[0, slot] * rows, rows)
            scales = jnp.zeros((16, LANES), jnp.int32)
            for t in range(depth):
                column = pl.multiple_of(meta[1 + t, slot] * LANES, LANES)
                packed, code = pack_tile(total[pl.ds(first, rows), pl.ds(column, LANES)])
                out[t * rows : (t + 1) * rows, :] = packed
                scales = jnp.where(line == t, code, scales)
            out[depth * rows : depth * rows + 16, :] = scales.astype(jnp.int16)


def score(meta, flat, done, pieces, order, depth):
    slots = len(order)
    height = depth * LANES + 16
    columns = sum(piece.shape[0] for piece in pieces)
    tall, width = flat.shape
    return pl.pallas_call(
        functools.partial(score_kernel, len(pieces), order, depth),
        grid=(width // DEPTH,),
        out_shape=[jax.ShapeDtypeStruct((height, LANES), jnp.int16)] * slots,
        in_specs=[
            pl.BlockSpec(memory_space=pltpu.SMEM),
            piece_spec(flat),
            pl.BlockSpec(done.shape, lambda k: (0, 0)),
        ]
        + [piece_spec(piece) for piece in pieces],
        out_specs=[pl.BlockSpec((height, LANES), lambda k: (0, 0))] * slots,
        scratch_shapes=[pltpu.VMEM((tall, done.shape[1] + columns), jnp.float32)],
        compiler_params=pltpu.CompilerParams(
            vmem_limit_bytes=48 * 2**20, dimension_semantics=("arbitrary",)
        ),
        cost_estimate=pl.CostEstimate(
            flops=2 * flat.size * columns,
            bytes_accessed=2 * (tall + columns) * width + 4 * done.size + 2 * slots * height * LANES,
            transcendentals=0,
        ),
        name="score",
    )(meta, flat, done, *pieces)


def unpack_kernel(order, depth, where, codes, *refs):
    out, stage, sems = refs[-3:]
    slots = len(order)
    step = pl.program_id(0)
    rows = LANES

    @pl.when(step == 0)
    def _():
        places = list(order) + [slots + slot for slot in order]
        copies = [
            pltpu.make_async_copy(message, stage.at[place], sems.at[place]) for place, message in zip(places, refs)
        ]
        for copy in copies:
            copy.start()
        for copy in copies:
            copy.wait()

    shard = where[0] + where[1] - step
    piece = step // 2
    first = pl.multiple_of(piece * rows, rows)
    line = lax.broadcasted_iota(jnp.int32, (16, LANES), 0)
    for pair in range(out.shape[1]):
        slot = codes[step, pair]
        index = slot + slots * lax.rem(where[0] + 1 + slot + shard, 2)
        tile = stage[index, pl.ds(first, rows), :].astype(jnp.int32).astype(jnp.float32)
        scale = stage[index, depth * rows : depth * rows + 16, :].astype(jnp.int32)
        scale = jnp.max(jnp.where(line == piece, scale, -(2**15)), axis=0, keepdims=True)
        out[0, pair] = tile * (jnp.exp2(scale.astype(jnp.float32) * (1.0 / OCTAVE)) * (1.0 / TOP))


def unpack(messages, where, codes, depth, order, steps):
    pairs = codes.shape[1]
    height = depth * LANES + 16
    smem = pl.BlockSpec(memory_space=pltpu.SMEM)
    return pl.pallas_call(
        functools.partial(unpack_kernel, order, depth),
        grid=(steps,),
        out_shape=jax.ShapeDtypeStruct((steps, pairs, LANES, LANES), jnp.float32),
        in_specs=[smem, smem] + [pl.BlockSpec(memory_space=pl.ANY)] * len(messages),
        out_specs=pl.BlockSpec((1, pairs, LANES, LANES), lambda step: (step, 0, 0, 0)),
        scratch_shapes=[
            pltpu.VMEM((len(messages), height, LANES), jnp.int16),
            pltpu.SemaphoreType.DMA((len(messages),)),
        ],
        compiler_params=pltpu.CompilerParams(
            vmem_limit_bytes=32 * 2**20, dimension_semantics=("arbitrary",)
        ),
        cost_estimate=pl.CostEstimate(
            flops=steps * pairs * LANES * LANES * 2, bytes_accessed=steps * pairs * LANES * LANES * 6, transcendentals=0
        ),
        name="unpack",
    )(where, codes, *messages)


def ring_place(chip, chips):
    return jnp.where(chip % 2 == 0, chip // 2, chips - 1 - chip // 2)


def per_device(cache, queries, plan, pair_codes):
    count = lax.axis_size("blk")
    myself = lax.axis_index("blk").astype(jnp.int32)
    local_blocks, rows, width = cache.shape
    slots = plan.shape[1]
    steps = pair_codes.shape[1]
    depth = steps // 2
    chips = count // 2
    core = myself % 2
    place = ring_place(myself // 2, chips)
    ring = list(range(0, chips, 2)) + list(range(chips - 1, 0, -2))
    hops = jnp.arange(1, slots + 1, dtype=jnp.int32)

    def meta_of(holder):
        served = (holder - hops) % count
        lines = [plan[served, hops - 1] - holder * local_blocks]
        for t in range(depth):
            shard = (served - (served - core) % 2 - 2 * t) % count
            away = (place - ring_place(shard // 2, chips)) % chips
            last = jnp.where(away == 1, chips - 2, chips - 1)
            lines.append(jnp.where(away == 0, 0, jnp.where((away == 1) | (away == chips - 1), last, away - 1)))
        return jnp.stack(lines)

    def hop(x, by):
        pairs = [
            (2 * ring[p] + k, 2 * ring[(p + by) % chips] + k) for p in range(chips) for k in range(2)
        ]
        return lax.ppermute(x, "blk", pairs)

    part = rows // PARTS
    way = [1] * (PARTS // 2) + [-1] * (PARTS // 2)
    turns = [q for pair in zip(range(PARTS // 2), range(PARTS // 2, PARTS)) for q in pair]
    held = [[queries[q * part : (q + 1) * part]] for q in range(PARTS)]
    flat = cache.reshape(local_blocks * rows, width)
    for _ in range(chips - 1):
        for q in turns:
            held[q].append(hop(held[q][-1], way[q]))
    sibling = lax.ppermute(flat, "blk", [(d, d ^ 1) for d in range(count)])

    def shard_pieces(away):
        return [held[q][away if way[q] > 0 else (chips - away) % chips] for q in range(PARTS)]

    first = [queries] + [piece for away in range(2, chips - 1) for piece in shard_pieces(away)]
    final = shard_pieces(1) + shard_pieces(chips - 1)

    order = [slot for pair in zip(reversed(range(slots)), range(slots)) for slot in pair][:slots]
    assert sorted(order) == list(range(slots))
    done = lax.optimization_barrier([early(blocks, first) for blocks in (flat, sibling)])
    received = []
    for other, blocks in enumerate((flat, sibling)):
        packed = score(meta_of(myself ^ other), blocks, done[other], final, order, depth)
        for slot, tiles in zip(order, packed):
            received.append(lax.ppermute(tiles, "blk", [(d, ((d ^ other) - slot - 1) % count) for d in range(count)]))
    where = jnp.stack([myself, jnp.int32(count)])
    return unpack(received, where, pair_codes[0], depth, order, steps)[None]


def solution(mesh):
    placed = (
        P(("groups", "blk"), None, None),
        P(("groups", "blk"), None),
        P("groups", None),
        P(("groups", "blk"), None, None),
    )
    return jax.shard_map(
        per_device,
        mesh=mesh,
        in_specs=placed,
        out_specs=P(("groups", "blk"), None, None, None, None),
        check_vma=False,
    )
```

```python
import functools

import jax
import jax.numpy as jnp
from jax import lax
from jax.experimental import pallas as pl
from jax.experimental.pallas import tpu as pltpu
from jax.sharding import PartitionSpec as P

LANES = 128
TOP = 32760.0
OCTAVE = 64.0
FLOOR = 2.0**-110
DEPTH = 2048
PARTS = 4


def pack_tile(x):
    peak = jnp.max(jnp.abs(x), axis=0, keepdims=True)
    code = jnp.ceil(jnp.log2(jnp.maximum(peak, FLOOR)) * OCTAVE)
    x = x * (jnp.exp2(code * (-1.0 / OCTAVE)) * TOP)
    x = jnp.clip(jnp.round(x), -32767.0, 32767.0)
    return x.astype(jnp.int32).astype(jnp.int16), code.astype(jnp.int32)


def multiply(cache, pieces):
    rows = jnp.concatenate([piece[...] for piece in pieces], axis=0)
    return lax.dot_general(cache[...], rows, (((1,), (1,)), ((), ())), preferred_element_type=jnp.float32)


def early_kernel(cache, *refs):
    pieces, out = refs[:-1], refs[-1]
    fresh = multiply(cache, pieces)

    @pl.when(pl.program_id(0) == 0)
    def _():
        out[...] = fresh

    @pl.when(pl.program_id(0) > 0)
    def _():
        out[...] += fresh


def piece_spec(piece):
    return pl.BlockSpec((piece.shape[0], DEPTH), lambda k: (0, k))


def early(flat, pieces):
    columns = sum(piece.shape[0] for piece in pieces)
    height, width = flat.shape
    return pl.pallas_call(
        early_kernel,
        grid=(width // DEPTH,),
        out_shape=jax.ShapeDtypeStruct((height, columns), jnp.float32),
        in_specs=[piece_spec(flat)] + [piece_spec(piece) for piece in pieces],
        out_specs=pl.BlockSpec((height, columns), lambda k: (0, 0)),
        compiler_params=pltpu.CompilerParams(
            vmem_limit_bytes=48 * 2**20, dimension_semantics=("arbitrary",)
        ),
        cost_estimate=pl.CostEstimate(
            flops=2 * flat.size * columns, bytes_accessed=2 * (height + columns) * width, transcendentals=0
        ),
        name="early",
    )(flat, *pieces)


def score_kernel(parts, count, order, depth, meta, cache, *refs):
    done, pieces, outs, total = refs[:parts], refs[parts : parts + count], refs[parts + count : -1], refs[-1]
    k = pl.program_id(0)
    rows = LANES
    each = done[0].shape[1]
    have = parts * each
    fresh = multiply(cache, pieces)

    @pl.when(k == 0)
    def _():
        for index, part in enumerate(done):
            total[:, index * each : (index + 1) * each] = part[...]
        total[:, have:] = fresh

    @pl.when(k > 0)
    def _():
        total[:, have:] += fresh

    @pl.when(k == pl.num_programs(0) - 1)
    def _():
        line = lax.broadcasted_iota(jnp.int32, (16, LANES), 0)
        for slot, out in zip(order, outs):
            first = pl.multiple_of(meta[0, slot] * rows, rows)
            scales = jnp.zeros((16, LANES), jnp.int32)
            for t in range(depth):
                column = pl.multiple_of(meta[1 + t, slot] * LANES, LANES)
                packed, code = pack_tile(total[pl.ds(first, rows), pl.ds(column, LANES)])
                out[t * rows : (t + 1) * rows, :] = packed
                scales = jnp.where(line == t, code, scales)
            out[depth * rows : depth * rows + 16, :] = scales.astype(jnp.int16)


def score(meta, flat, done, pieces, order, depth):
    slots = len(order)
    height = depth * LANES + 16
    columns = sum(piece.shape[0] for piece in pieces)
    tall, width = flat.shape
    return pl.pallas_call(
        functools.partial(score_kernel, len(done), len(pieces), order, depth),
        grid=(width // DEPTH,),
        out_shape=[jax.ShapeDtypeStruct((height, LANES), jnp.int16)] * slots,
        in_specs=[
            pl.BlockSpec(memory_space=pltpu.SMEM),
            piece_spec(flat),
        ]
        + [pl.BlockSpec(part.shape, lambda k: (0, 0)) for part in done]
        + [piece_spec(piece) for piece in pieces],
        out_specs=[pl.BlockSpec((height, LANES), lambda k: (0, 0))] * slots,
        scratch_shapes=[pltpu.VMEM((tall, sum(part.shape[1] for part in done) + columns), jnp.float32)],
        compiler_params=pltpu.CompilerParams(
            vmem_limit_bytes=48 * 2**20, dimension_semantics=("arbitrary",)
        ),
        cost_estimate=pl.CostEstimate(
            flops=2 * flat.size * columns,
            bytes_accessed=2 * (tall + columns) * width + 4 * sum(part.size for part in done) + 2 * slots * height * LANES,
            transcendentals=0,
        ),
        name="score",
    )(meta, flat, *done, *pieces)


def unpack_kernel(order, depth, where, codes, *refs):
    out, stage, factors, sems = refs[-4:]
    slots = len(order)
    step = pl.program_id(0)
    rows = LANES

    @pl.when(step == 0)
    def _():
        places = list(order) + [slots + slot for slot in order]
        copies = [
            pltpu.make_async_copy(message, stage.at[place], sems.at[place]) for place, message in zip(places, refs)
        ]
        for copy in copies:
            copy.start()
        for copy in copies:
            copy.wait()

        for place in places:
            codes_of = stage[place, depth * rows : depth * rows + 16, :].astype(jnp.int32).astype(jnp.float32)
            factors[place] = jnp.exp2(codes_of * (1.0 / OCTAVE)) * (1.0 / TOP)

    shard = where[0] + where[1] - step
    piece = step // 2
    first = pl.multiple_of(piece * rows, rows)
    for pair in range(out.shape[1]):
        slot = codes[step, pair]
        index = slot + slots * lax.rem(where[0] + 1 + slot + shard, 2)
        tile = stage[index, pl.ds(first, rows), :].astype(jnp.int32).astype(jnp.float32)
        out[0, pair] = tile * factors[index, pl.ds(piece, 1), :]


def unpack(messages, where, codes, depth, order, steps):
    pairs = codes.shape[1]
    height = depth * LANES + 16
    smem = pl.BlockSpec(memory_space=pltpu.SMEM)
    return pl.pallas_call(
        functools.partial(unpack_kernel, order, depth),
        grid=(steps,),
        out_shape=jax.ShapeDtypeStruct((steps, pairs, LANES, LANES), jnp.float32),
        in_specs=[smem, smem] + [pl.BlockSpec(memory_space=pl.ANY)] * len(messages),
        out_specs=pl.BlockSpec((1, pairs, LANES, LANES), lambda step: (step, 0, 0, 0)),
        scratch_shapes=[
            pltpu.VMEM((len(messages), height, LANES), jnp.int16),
            pltpu.VMEM((len(messages), 16, LANES), jnp.float32),
            pltpu.SemaphoreType.DMA((len(messages),)),
        ],
        compiler_params=pltpu.CompilerParams(
            vmem_limit_bytes=32 * 2**20, dimension_semantics=("arbitrary",)
        ),
        cost_estimate=pl.CostEstimate(
            flops=steps * pairs * LANES * LANES * 2, bytes_accessed=steps * pairs * LANES * LANES * 6, transcendentals=0
        ),
        name="unpack",
    )(where, codes, *messages)


def ring_place(chip, chips):
    return jnp.where(chip % 2 == 0, chip // 2, chips - 1 - chip // 2)


def per_device(cache, queries, plan, pair_codes):
    count = lax.axis_size("blk")
    myself = lax.axis_index("blk").astype(jnp.int32)
    local_blocks, rows, width = cache.shape
    slots = plan.shape[1]
    steps = pair_codes.shape[1]
    depth = steps // 2
    chips = count // 2
    half = chips // 2
    core = myself % 2
    place = ring_place(myself // 2, chips)
    ring = list(range(0, chips, 2)) + list(range(chips - 1, 0, -2))
    hops = jnp.arange(1, slots + 1, dtype=jnp.int32)

    def meta_of(holder):
        served = (holder - hops) % count
        lines = [plan[served, hops - 1] - holder * local_blocks]
        for t in range(depth):
            shard = (served - (served - core) % 2 - 2 * t) % count
            away = (place - ring_place(shard // 2, chips)) % chips
            pair = 2 * jnp.abs(away - half) + jnp.where(away > half, 1, 0)
            lines.append(jnp.where(away == 0, 0, jnp.where(away == half, 1, pair)))
        return jnp.stack(lines)

    def hop(x, by):
        pairs = [
            (2 * ring[p] + k, 2 * ring[(p + by) % chips] + k) for p in range(chips) for k in range(2)
        ]
        return lax.ppermute(x, "blk", pairs)

    part = rows // PARTS
    way = [1] * (PARTS // 2) + [-1] * (PARTS // 2)
    turns = [q for pair in zip(range(PARTS // 2), range(PARTS // 2, PARTS)) for q in pair]
    held = [[queries[q * part : (q + 1) * part]] for q in range(PARTS)]
    flat = cache.reshape(local_blocks * rows, width)
    sibling = lax.ppermute(flat, "blk", [(d, d ^ 1) for d in range(count)])
    sources = (flat, sibling)

    def shard_pieces(away):
        if away == 0:
            return [queries]
        return [held[q][away if way[q] > 0 else chips - away] for q in range(PARTS)]

    pairs = [(0, half)] + [(half - d, half + d) for d in range(1, half)]
    done = [[], []]
    for step in range(1, chips):
        ready = step - half - 2
        if ready >= 0:
            for other in range(2):
                q = turns[-1 - other]
                held[q][-1], done[other][ready] = lax.optimization_barrier((held[q][-1], done[other][ready]))
        for q in turns:
            held[q].append(hop(held[q][-1], way[q]))
        if half <= step < chips - 1:
            pieces = [piece for away in pairs[step - half] for piece in shard_pieces(away)]
            for other, blocks in enumerate(sources):
                done[other].append(early(blocks, pieces))
    final = [piece for away in pairs[-1] for piece in shard_pieces(away)]
    done = lax.optimization_barrier(done)

    order = [slot for pair in zip(reversed(range(slots)), range(slots)) for slot in pair][:slots]
    assert sorted(order) == list(range(slots))
    received = []
    for other, blocks in enumerate(sources):
        packed = score(meta_of(myself ^ other), blocks, done[other], final, order, depth)
        for slot, tiles in zip(order, packed):
            received.append(lax.ppermute(tiles, "blk", [(d, ((d ^ other) - slot - 1) % count) for d in range(count)]))
    where = jnp.stack([myself, jnp.int32(count)])
    return unpack(received, where, pair_codes[0], depth, order, steps)[None]


def solution(mesh):
    placed = (
        P(("groups", "blk"), None, None),
        P(("groups", "blk"), None),
        P("groups", None),
        P(("groups", "blk"), None, None),
    )
    return jax.shard_map(
        per_device,
        mesh=mesh,
        in_specs=placed,
        out_specs=P(("groups", "blk"), None, None, None, None),
        check_vma=False,
    )
```

```python
import functools

import jax
import jax.numpy as jnp
from jax import lax
from jax.experimental import pallas as pl
from jax.experimental.pallas import tpu as pltpu
from jax.sharding import PartitionSpec as P

LANES = 128
TOP = 32760.0
OCTAVE = 64.0
FLOOR = 2.0**-110
DEPTH = 2048
PARTS = 4


def pack_tile(x):
    peak = jnp.max(jnp.abs(x), axis=0, keepdims=True)
    code = jnp.ceil(jnp.log2(jnp.maximum(peak, FLOOR)) * OCTAVE)
    x = x * (jnp.exp2(code * (-1.0 / OCTAVE)) * TOP)
    x = jnp.clip(jnp.round(x), -32767.0, 32767.0)
    return x.astype(jnp.int32).astype(jnp.int16), code.astype(jnp.int32)


def multiply(cache, pieces):
    rows = jnp.concatenate([piece[...] for piece in pieces], axis=0)
    return lax.dot_general(cache[...], rows, (((1,), (1,)), ((), ())), preferred_element_type=jnp.float32)


def early_kernel(cache, *refs):
    pieces, out = refs[:-1], refs[-1]
    fresh = multiply(cache, pieces)

    @pl.when(pl.program_id(0) == 0)
    def _():
        out[...] = fresh

    @pl.when(pl.program_id(0) > 0)
    def _():
        out[...] += fresh


def piece_spec(piece):
    return pl.BlockSpec((piece.shape[0], DEPTH), lambda k: (0, k))


def early(flat, pieces):
    columns = sum(piece.shape[0] for piece in pieces)
    height, width = flat.shape
    return pl.pallas_call(
        early_kernel,
        grid=(width // DEPTH,),
        out_shape=jax.ShapeDtypeStruct((height, columns), jnp.float32),
        in_specs=[piece_spec(flat)] + [piece_spec(piece) for piece in pieces],
        out_specs=pl.BlockSpec((height, columns), lambda k: (0, 0)),
        compiler_params=pltpu.CompilerParams(
            vmem_limit_bytes=48 * 2**20, dimension_semantics=("arbitrary",)
        ),
        cost_estimate=pl.CostEstimate(
            flops=2 * flat.size * columns, bytes_accessed=2 * (height + columns) * width, transcendentals=0
        ),
        name="early",
    )(flat, *pieces)


def score_kernel(parts, count, order, depth, meta, cache, *refs):
    done, pieces, outs, total = refs[:parts], refs[parts : parts + count], refs[parts + count : -1], refs[-1]
    k = pl.program_id(0)
    rows = LANES
    each = done[0].shape[1]
    have = parts * each
    fresh = multiply(cache, pieces)

    @pl.when(k == 0)
    def _():
        for index, part in enumerate(done):
            total[:, index * each : (index + 1) * each] = part[...]
        total[:, have:] = fresh

    @pl.when(k > 0)
    def _():
        total[:, have:] += fresh

    @pl.when(k == pl.num_programs(0) - 1)
    def _():
        line = lax.broadcasted_iota(jnp.int32, (16, LANES), 0)
        for slot, out in zip(order, outs):
            first = pl.multiple_of(meta[0, slot] * rows, rows)
            scales = jnp.zeros((16, LANES), jnp.int32)
            for t in range(depth):
                column = pl.multiple_of(meta[1 + t, slot] * LANES, LANES)
                packed, code = pack_tile(total[pl.ds(first, rows), pl.ds(column, LANES)])
                out[t * rows : (t + 1) * rows, :] = packed
                scales = jnp.where(line == t, code, scales)
            out[depth * rows : depth * rows + 16, :] = scales.astype(jnp.int16)


def score(meta, flat, done, pieces, order, depth):
    slots = len(order)
    height = depth * LANES + 16
    columns = sum(piece.shape[0] for piece in pieces)
    tall, width = flat.shape
    return pl.pallas_call(
        functools.partial(score_kernel, len(done), len(pieces), order, depth),
        grid=(width // DEPTH,),
        out_shape=[jax.ShapeDtypeStruct((height, LANES), jnp.int16)] * slots,
        in_specs=[
            pl.BlockSpec(memory_space=pltpu.SMEM),
            piece_spec(flat),
        ]
        + [pl.BlockSpec(part.shape, lambda k: (0, 0)) for part in done]
        + [piece_spec(piece) for piece in pieces],
        out_specs=[pl.BlockSpec((height, LANES), lambda k: (0, 0))] * slots,
        scratch_shapes=[pltpu.VMEM((tall, sum(part.shape[1] for part in done) + columns), jnp.float32)],
        compiler_params=pltpu.CompilerParams(
            vmem_limit_bytes=48 * 2**20, dimension_semantics=("arbitrary",)
        ),
        cost_estimate=pl.CostEstimate(
            flops=2 * flat.size * columns,
            bytes_accessed=2 * (tall + columns) * width + 4 * sum(part.size for part in done) + 2 * slots * height * LANES,
            transcendentals=0,
        ),
        name="score",
    )(meta, flat, *done, *pieces)


def unpack_kernel(group, order, depth, where, codes, *refs):
    out, stage, factors, tiles, arrived, written = refs[-6:]
    steps, pairs = out.shape[:2]
    rows = LANES
    copies = [pltpu.make_async_copy(message, stage.at[slot], arrived.at[slot]) for slot, message in zip(order, refs)]
    for copy in copies:
        copy.start()
    for copy in copies:
        copy.wait()
    for slot in order:
        codes_of = stage[slot, depth * rows : depth * rows + 16, :].astype(jnp.int32).astype(jnp.float32)
        factors[slot] = jnp.exp2(codes_of * (1.0 / OCTAVE)) * (1.0 / TOP)

    def each(body):
        def one(step, carry):
            shard = where[0] + where[1] - step
            for pair in range(pairs):
                slot = codes[step, pair]
                place = step * pairs + pair
                copy = pltpu.make_async_copy(tiles.at[place], out.at[step, pair], written.at[place])
                pl.when(lax.rem(where[0] + 1 + slot + shard, 2) == group)(
                    functools.partial(body, step, slot, place, copy)
                )
            return carry

        lax.fori_loop(0, steps, one, 0)

    def write(step, slot, place, copy):
        piece = step // 2
        first = pl.multiple_of(piece * rows, rows)
        tile = stage[slot, pl.ds(first, rows), :].astype(jnp.int32).astype(jnp.float32)
        tiles[place] = tile * factors[slot, pl.ds(piece, 1), :]
        copy.start()

    def finish(step, slot, place, copy):
        copy.wait()

    each(write)
    each(finish)


def unpack(messages, where, codes, group, depth, order, steps, before=None):
    pairs = codes.shape[1]
    slots = len(order)
    height = depth * LANES + 16
    smem = pl.BlockSpec(memory_space=pltpu.SMEM)
    operands = [where, codes, *messages] + ([] if before is None else [before])
    return pl.pallas_call(
        functools.partial(unpack_kernel, group, order, depth),
        out_shape=jax.ShapeDtypeStruct((steps, pairs, LANES, LANES), jnp.float32),
        in_specs=[smem, smem] + [pl.BlockSpec(memory_space=pl.ANY)] * (len(operands) - 2),
        out_specs=pl.BlockSpec(memory_space=pl.ANY),
        scratch_shapes=[
            pltpu.VMEM((slots, height, LANES), jnp.int16),
            pltpu.VMEM((slots, 16, LANES), jnp.float32),
            pltpu.VMEM((steps * pairs, LANES, LANES), jnp.float32),
            pltpu.SemaphoreType.DMA((slots,)),
            pltpu.SemaphoreType.DMA((steps * pairs,)),
        ],
        input_output_aliases={} if before is None else {len(operands) - 1: 0},
        compiler_params=pltpu.CompilerParams(vmem_limit_bytes=32 * 2**20),
        cost_estimate=pl.CostEstimate(
            flops=steps * pairs * LANES * LANES, bytes_accessed=steps * pairs * LANES * LANES * 3, transcendentals=0
        ),
        name="unpack",
    )(*operands)


def ring_place(chip, chips):
    return jnp.where(chip % 2 == 0, chip // 2, chips - 1 - chip // 2)


def per_device(cache, queries, plan, pair_codes):
    count = lax.axis_size("blk")
    myself = lax.axis_index("blk").astype(jnp.int32)
    local_blocks, rows, width = cache.shape
    slots = plan.shape[1]
    steps = pair_codes.shape[1]
    depth = steps // 2
    chips = count // 2
    half = chips // 2
    core = myself % 2
    place = ring_place(myself // 2, chips)
    ring = list(range(0, chips, 2)) + list(range(chips - 1, 0, -2))
    hops = jnp.arange(1, slots + 1, dtype=jnp.int32)

    def meta_of(holder):
        served = (holder - hops) % count
        lines = [plan[served, hops - 1] - holder * local_blocks]
        for t in range(depth):
            shard = (served - (served - core) % 2 - 2 * t) % count
            away = (place - ring_place(shard // 2, chips)) % chips
            pair = 2 * jnp.abs(away - half) + jnp.where(away > half, 1, 0)
            lines.append(jnp.where(away == 0, 0, jnp.where(away == half, 1, pair)))
        return jnp.stack(lines)

    def hop(x, by):
        pairs = [
            (2 * ring[p] + k, 2 * ring[(p + by) % chips] + k) for p in range(chips) for k in range(2)
        ]
        return lax.ppermute(x, "blk", pairs)

    part = rows // PARTS
    way = [1] * (PARTS // 2) + [-1] * (PARTS // 2)
    turns = [q for pair in zip(range(PARTS // 2), range(PARTS // 2, PARTS)) for q in pair]
    held = [[queries[q * part : (q + 1) * part]] for q in range(PARTS)]
    flat = cache.reshape(local_blocks * rows, width)
    sibling = lax.ppermute(flat, "blk", [(d, d ^ 1) for d in range(count)])
    sources = (flat, sibling)

    def shard_pieces(away):
        if away == 0:
            return [queries]
        return [held[q][away if way[q] > 0 else chips - away] for q in range(PARTS)]

    pairs = [(0, half)] + [(half - d, half + d) for d in range(1, half)]
    done = [[], []]
    for step in range(1, chips):
        ready = step - half - 2
        if ready >= 0:
            for other in range(2):
                q = turns[-1 - other]
                held[q][-1], done[other][ready] = lax.optimization_barrier((held[q][-1], done[other][ready]))
        for q in turns:
            held[q].append(hop(held[q][-1], way[q]))
        if half <= step < chips - 1:
            pieces = [piece for away in pairs[step - half] for piece in shard_pieces(away)]
            for other, blocks in enumerate(sources):
                done[other].append(early(blocks, pieces))
    final = [piece for away in pairs[-1] for piece in shard_pieces(away)]
    done = lax.optimization_barrier(done)

    order = [slot for pair in zip(reversed(range(slots)), range(slots)) for slot in pair][:slots]
    assert sorted(order) == list(range(slots))
    received = []
    for other, blocks in enumerate(sources):
        packed = score(meta_of(myself ^ other), blocks, done[other], final, order, depth)
        received.append(
            [
                lax.ppermute(tiles, "blk", [(d, ((d ^ other) - slot - 1) % count) for d in range(count)])
                for slot, tiles in zip(order, packed)
            ]
        )
    where = jnp.stack([myself, jnp.int32(count)])
    scores = None
    for other in range(2):
        scores = unpack(received[other], where, pair_codes[0], other, depth, order, steps, scores)
    return scores[None]


def solution(mesh):
    placed = (
        P(("groups", "blk"), None, None),
        P(("groups", "blk"), None),
        P("groups", None),
        P(("groups", "blk"), None, None),
    )
    return jax.shard_map(
        per_device,
        mesh=mesh,
        in_specs=placed,
        out_specs=P(("groups", "blk"), None, None, None, None),
        check_vma=False,
    )
```

```python
import functools

import jax
import jax.numpy as jnp
from jax import lax
from jax.experimental import pallas as pl
from jax.experimental.pallas import tpu as pltpu
from jax.sharding import PartitionSpec as P

LANES = 128
TOP = 32760.0
OCTAVE = 64.0
FLOOR = 2.0**-110
DEPTH = 2048
PARTS = 4


def pack_tile(x):
    peak = jnp.max(jnp.abs(x), axis=0, keepdims=True)
    code = jnp.ceil(jnp.log2(jnp.maximum(peak, FLOOR)) * OCTAVE)
    x = x * (jnp.exp2(code * (-1.0 / OCTAVE)) * TOP)
    x = jnp.clip(jnp.round(x), -32767.0, 32767.0)
    return x.astype(jnp.int32).astype(jnp.int16), code.astype(jnp.int32)


def multiply(cache, pieces):
    rows = jnp.concatenate([piece[...] for piece in pieces], axis=0)
    return lax.dot_general(cache[...], rows, (((1,), (1,)), ((), ())), preferred_element_type=jnp.float32)


def early_kernel(cache, *refs):
    pieces, out = refs[:-1], refs[-1]
    fresh = multiply(cache, pieces)

    @pl.when(pl.program_id(0) == 0)
    def _():
        out[...] = fresh

    @pl.when(pl.program_id(0) > 0)
    def _():
        out[...] += fresh


def piece_spec(piece):
    return pl.BlockSpec((piece.shape[0], DEPTH), lambda k: (0, k))


def early(flat, pieces):
    columns = sum(piece.shape[0] for piece in pieces)
    height, width = flat.shape
    return pl.pallas_call(
        early_kernel,
        grid=(width // DEPTH,),
        out_shape=jax.ShapeDtypeStruct((height, columns), jnp.float32),
        in_specs=[piece_spec(flat)] + [piece_spec(piece) for piece in pieces],
        out_specs=pl.BlockSpec((height, columns), lambda k: (0, 0)),
        compiler_params=pltpu.CompilerParams(
            vmem_limit_bytes=16 * 2**20, dimension_semantics=("arbitrary",)
        ),
        cost_estimate=pl.CostEstimate(
            flops=2 * flat.size * columns, bytes_accessed=2 * (height + columns) * width, transcendentals=0
        ),
        name="early",
    )(flat, *pieces)


def score_kernel(parts, count, order, depth, meta, cache, *refs):
    done, pieces, outs, total = refs[:parts], refs[parts : parts + count], refs[parts + count : -1], refs[-1]
    k = pl.program_id(0)
    rows = LANES
    each = done[0].shape[1]
    have = parts * each
    fresh = multiply(cache, pieces)

    @pl.when(k == 0)
    def _():
        for index, part in enumerate(done):
            total[:, index * each : (index + 1) * each] = part[...]
        total[:, have:] = fresh

    @pl.when(k > 0)
    def _():
        total[:, have:] += fresh

    @pl.when(k == pl.num_programs(0) - 1)
    def _():
        line = lax.broadcasted_iota(jnp.int32, (16, LANES), 0)
        for slot, out in zip(order, outs):
            first = pl.multiple_of(meta[0, slot] * rows, rows)
            scales = jnp.zeros((16, LANES), jnp.int32)
            for t in range(depth):
                column = pl.multiple_of(meta[1 + t, slot] * LANES, LANES)
                packed, code = pack_tile(total[pl.ds(first, rows), pl.ds(column, LANES)])
                out[t * rows : (t + 1) * rows, :] = packed
                scales = jnp.where(line == t, code, scales)
            out[depth * rows : depth * rows + 16, :] = scales.astype(jnp.int16)


def score(meta, flat, done, pieces, order, depth):
    slots = len(order)
    height = depth * LANES + 16
    columns = sum(piece.shape[0] for piece in pieces)
    tall, width = flat.shape
    return pl.pallas_call(
        functools.partial(score_kernel, len(done), len(pieces), order, depth),
        grid=(width // DEPTH,),
        out_shape=[jax.ShapeDtypeStruct((height, LANES), jnp.int16)] * slots,
        in_specs=[
            pl.BlockSpec(memory_space=pltpu.SMEM),
            piece_spec(flat),
        ]
        + [pl.BlockSpec(part.shape, lambda k: (0, 0)) for part in done]
        + [piece_spec(piece) for piece in pieces],
        out_specs=[pl.BlockSpec((height, LANES), lambda k: (0, 0))] * slots,
        scratch_shapes=[pltpu.VMEM((tall, sum(part.shape[1] for part in done) + columns), jnp.float32)],
        compiler_params=pltpu.CompilerParams(
            vmem_limit_bytes=32 * 2**20, dimension_semantics=("arbitrary",)
        ),
        cost_estimate=pl.CostEstimate(
            flops=2 * flat.size * columns,
            bytes_accessed=2 * (tall + columns) * width + 4 * sum(part.size for part in done) + 2 * slots * height * LANES,
            transcendentals=0,
        ),
        name="score",
    )(meta, flat, *done, *pieces)


def unpack_kernel(group, order, depth, where, codes, *refs):
    out, stage, factors, tiles, arrived, written = refs[-6:]
    steps, pairs = out.shape[:2]
    rows = LANES
    copies = [pltpu.make_async_copy(message, stage.at[slot], arrived.at[slot]) for slot, message in zip(order, refs)]
    for copy in copies:
        copy.start()
    for copy in copies:
        copy.wait()
    for slot in order:
        codes_of = stage[slot, depth * rows : depth * rows + 16, :].astype(jnp.int32).astype(jnp.float32)
        factors[slot] = jnp.exp2(codes_of * (1.0 / OCTAVE)) * (1.0 / TOP)

    def each(body):
        def one(step, carry):
            shard = where[0] + where[1] - step
            for pair in range(pairs):
                slot = codes[step, pair]
                place = step * pairs + pair
                copy = pltpu.make_async_copy(tiles.at[place], out.at[step, pair], written.at[place])
                pl.when(lax.rem(where[0] + 1 + slot + shard, 2) == group)(
                    functools.partial(body, step, slot, place, copy)
                )
            return carry

        lax.fori_loop(0, steps, one, 0)

    def write(step, slot, place, copy):
        piece = step // 2
        first = pl.multiple_of(piece * rows, rows)
        tile = stage[slot, pl.ds(first, rows), :].astype(jnp.int32).astype(jnp.float32)
        tiles[place] = tile * factors[slot, pl.ds(piece, 1), :]
        copy.start()

    def finish(step, slot, place, copy):
        copy.wait()

    each(write)
    each(finish)


def unpack(messages, where, codes, group, depth, order, steps, before=None):
    pairs = codes.shape[1]
    slots = len(order)
    height = depth * LANES + 16
    smem = pl.BlockSpec(memory_space=pltpu.SMEM)
    operands = [where, codes, *messages] + ([] if before is None else [before])
    return pl.pallas_call(
        functools.partial(unpack_kernel, group, order, depth),
        out_shape=jax.ShapeDtypeStruct((steps, pairs, LANES, LANES), jnp.float32),
        in_specs=[smem, smem] + [pl.BlockSpec(memory_space=pl.ANY)] * (len(operands) - 2),
        out_specs=pl.BlockSpec(memory_space=pl.ANY),
        scratch_shapes=[
            pltpu.VMEM((slots, height, LANES), jnp.int16),
            pltpu.VMEM((slots, 16, LANES), jnp.float32),
            pltpu.VMEM((steps * pairs, LANES, LANES), jnp.float32),
            pltpu.SemaphoreType.DMA((slots,)),
            pltpu.SemaphoreType.DMA((steps * pairs,)),
        ],
        input_output_aliases={} if before is None else {len(operands) - 1: 0},
        compiler_params=pltpu.CompilerParams(vmem_limit_bytes=16 * 2**20),
        cost_estimate=pl.CostEstimate(
            flops=steps * pairs * LANES * LANES, bytes_accessed=steps * pairs * LANES * LANES * 3, transcendentals=0
        ),
        name="unpack",
    )(*operands)


def ring_place(chip, chips):
    return jnp.where(chip % 2 == 0, chip // 2, chips - 1 - chip // 2)


def per_device(cache, queries, plan, pair_codes):
    count = lax.axis_size("blk")
    myself = lax.axis_index("blk").astype(jnp.int32)
    local_blocks, rows, width = cache.shape
    slots = plan.shape[1]
    steps = pair_codes.shape[1]
    depth = steps // 2
    chips = count // 2
    half = chips // 2
    core = myself % 2
    place = ring_place(myself // 2, chips)
    ring = list(range(0, chips, 2)) + list(range(chips - 1, 0, -2))
    hops = jnp.arange(1, slots + 1, dtype=jnp.int32)

    def meta_of(holder):
        served = (holder - hops) % count
        lines = [plan[served, hops - 1] - holder * local_blocks]
        for t in range(depth):
            shard = (served - (served - core) % 2 - 2 * t) % count
            away = (place - ring_place(shard // 2, chips)) % chips
            pair = 2 * jnp.abs(away - half) + jnp.where(away > half, 1, 0)
            lines.append(jnp.where(away == 0, 0, jnp.where(away == half, 1, pair)))
        return jnp.stack(lines)

    def hop(x, by):
        pairs = [
            (2 * ring[p] + k, 2 * ring[(p + by) % chips] + k) for p in range(chips) for k in range(2)
        ]
        return lax.ppermute(x, "blk", pairs)

    part = rows // PARTS
    way = [1] * (PARTS // 2) + [-1] * (PARTS // 2)
    turns = [q for pair in zip(range(PARTS // 2), range(PARTS // 2, PARTS)) for q in pair]
    held = [[queries[q * part : (q + 1) * part]] for q in range(PARTS)]
    flat = cache.reshape(local_blocks * rows, width)
    sibling = lax.ppermute(flat, "blk", [(d, d ^ 1) for d in range(count)])
    sources = (flat, sibling)

    def shard_pieces(away):
        if away == 0:
            return [queries]
        return [held[q][away if way[q] > 0 else chips - away] for q in range(PARTS)]

    pairs = [(0, half)] + [(half - d, half + d) for d in range(1, half)]
    done = [[], []]
    for step in range(1, chips):
        ready = step - half - 2
        if ready >= 0:
            for other in range(2):
                q = turns[-1 - other]
                held[q][-1], done[other][ready] = lax.optimization_barrier((held[q][-1], done[other][ready]))
        for q in turns:
            held[q].append(hop(held[q][-1], way[q]))
        if half <= step < chips - 1:
            pieces = [piece for away in pairs[step - half] for piece in shard_pieces(away)]
            for other, blocks in enumerate(sources):
                done[other].append(early(blocks, pieces))
    final = [piece for away in pairs[-1] for piece in shard_pieces(away)]
    done = lax.optimization_barrier(done)

    order = [slot for pair in zip(reversed(range(slots)), range(slots)) for slot in pair][:slots]
    assert sorted(order) == list(range(slots))
    where = jnp.stack([myself, jnp.int32(count)])
    early_sends = slots // 2
    received, scores = [], None
    for other, blocks in enumerate(sources):
        packed = list(score(meta_of(myself ^ other), blocks, done[other], final, order, depth))
        if other:
            scores = unpack(received, where, pair_codes[0], 0, depth, order, steps)
            packed[early_sends:], scores = lax.optimization_barrier((packed[early_sends:], scores))
        received = [
            lax.ppermute(tiles, "blk", [(d, ((d ^ other) - slot - 1) % count) for d in range(count)])
            for slot, tiles in zip(order, packed)
        ]
    return unpack(received, where, pair_codes[0], 1, depth, order, steps, scores)[None]


def solution(mesh):
    placed = (
        P(("groups", "blk"), None, None),
        P(("groups", "blk"), None),
        P("groups", None),
        P(("groups", "blk"), None, None),
    )
    return jax.shard_map(
        per_device,
        mesh=mesh,
        in_specs=placed,
        out_specs=P(("groups", "blk"), None, None, None, None),
        check_vma=False,
    )
```

```python
import functools

import jax
import jax.numpy as jnp
from jax import lax
from jax.experimental import pallas as pl
from jax.experimental.pallas import tpu as pltpu
from jax.sharding import PartitionSpec as P

LANES = 128
TOP = 32760.0
OCTAVE = 64.0
FLOOR = 2.0**-110
DEPTH = 2048
PARTS = 4


def pack_tile(x):
    peak = jnp.max(jnp.abs(x), axis=0, keepdims=True)
    code = jnp.ceil(jnp.log2(jnp.maximum(peak, FLOOR)) * OCTAVE)
    x = x * (jnp.exp2(code * (-1.0 / OCTAVE)) * TOP)
    x = jnp.clip(jnp.round(x), -32767.0, 32767.0)
    return x.astype(jnp.int32).astype(jnp.int16), code.astype(jnp.int32)


def multiply(cache, pieces):
    rows = jnp.concatenate([piece[...] for piece in pieces], axis=0)
    return lax.dot_general(cache[...], rows, (((1,), (1,)), ((), ())), preferred_element_type=jnp.float32)


def early_kernel(cache, *refs):
    pieces, out = refs[:-1], refs[-1]
    fresh = multiply(cache, pieces)

    @pl.when(pl.program_id(0) == 0)
    def _():
        out[...] = fresh

    @pl.when(pl.program_id(0) > 0)
    def _():
        out[...] += fresh


def piece_spec(piece):
    return pl.BlockSpec((piece.shape[0], DEPTH), lambda k: (0, k))


def early(flat, pieces):
    columns = sum(piece.shape[0] for piece in pieces)
    height, width = flat.shape
    return pl.pallas_call(
        early_kernel,
        grid=(width // DEPTH,),
        out_shape=jax.ShapeDtypeStruct((height, columns), jnp.float32),
        in_specs=[piece_spec(flat)] + [piece_spec(piece) for piece in pieces],
        out_specs=pl.BlockSpec((height, columns), lambda k: (0, 0)),
        compiler_params=pltpu.CompilerParams(
            vmem_limit_bytes=16 * 2**20, dimension_semantics=("arbitrary",)
        ),
        cost_estimate=pl.CostEstimate(
            flops=2 * flat.size * columns, bytes_accessed=2 * (height + columns) * width, transcendentals=0
        ),
        name="early",
    )(flat, *pieces)


def score_kernel(parts, count, order, depth, meta, cache, *refs):
    done, pieces, outs, total = refs[:parts], refs[parts : parts + count], refs[parts + count : -1], refs[-1]
    k = pl.program_id(0)
    rows = LANES
    each = done[0].shape[1]
    have = parts * each
    fresh = multiply(cache, pieces)

    @pl.when(k == 0)
    def _():
        for index, part in enumerate(done):
            total[:, index * each : (index + 1) * each] = part[...]
        total[:, have:] = fresh

    @pl.when(k > 0)
    def _():
        total[:, have:] += fresh

    @pl.when(k == pl.num_programs(0) - 1)
    def _():
        line = lax.broadcasted_iota(jnp.int32, (16, LANES), 0)
        for slot, out in zip(order, outs):
            first = pl.multiple_of(meta[0, slot] * rows, rows)
            scales = jnp.zeros((16, LANES), jnp.int32)
            for t in range(depth):
                column = pl.multiple_of(meta[1 + t, slot] * LANES, LANES)
                packed, code = pack_tile(total[pl.ds(first, rows), pl.ds(column, LANES)])
                out[t * rows : (t + 1) * rows, :] = packed
                scales = jnp.where(line == t, code, scales)
            out[depth * rows : depth * rows + 16, :] = scales.astype(jnp.int16)


def score(meta, flat, done, pieces, order, depth, room):
    slots = len(order)
    height = depth * LANES + 16
    columns = sum(piece.shape[0] for piece in pieces)
    tall, width = flat.shape
    return pl.pallas_call(
        functools.partial(score_kernel, len(done), len(pieces), order, depth),
        grid=(width // DEPTH,),
        out_shape=[jax.ShapeDtypeStruct((height, LANES), jnp.int16)] * slots,
        in_specs=[
            pl.BlockSpec(memory_space=pltpu.SMEM),
            piece_spec(flat),
        ]
        + [pl.BlockSpec(part.shape, lambda k: (0, 0)) for part in done]
        + [piece_spec(piece) for piece in pieces],
        out_specs=[pl.BlockSpec((height, LANES), lambda k: (0, 0))] * slots,
        scratch_shapes=[pltpu.VMEM((tall, sum(part.shape[1] for part in done) + columns), jnp.float32)],
        compiler_params=pltpu.CompilerParams(
            vmem_limit_bytes=room * 2**20, dimension_semantics=("arbitrary",)
        ),
        cost_estimate=pl.CostEstimate(
            flops=2 * flat.size * columns,
            bytes_accessed=2 * (tall + columns) * width + 4 * sum(part.size for part in done) + 2 * slots * height * LANES,
            transcendentals=0,
        ),
        name="score",
    )(meta, flat, *done, *pieces)


def unpack_kernel(group, order, depth, where, codes, *refs):
    out, stage, factors, tiles, arrived, written = refs[-6:]
    steps, pairs = out.shape[:2]
    rows = LANES
    copies = [pltpu.make_async_copy(message, stage.at[slot], arrived.at[slot]) for slot, message in zip(order, refs)]
    for copy in copies:
        copy.start()
    for copy in copies:
        copy.wait()
    for slot in order:
        codes_of = stage[slot, depth * rows : depth * rows + 16, :].astype(jnp.int32).astype(jnp.float32)
        factors[slot] = jnp.exp2(codes_of * (1.0 / OCTAVE)) * (1.0 / TOP)

    def each(body):
        def one(step, carry):
            shard = where[0] + where[1] - step
            for pair in range(pairs):
                slot = codes[step, pair]
                place = step * pairs + pair
                copy = pltpu.make_async_copy(tiles.at[place], out.at[step, pair], written.at[place])
                pl.when(lax.rem(where[0] + 1 + slot + shard, 2) == group)(
                    functools.partial(body, step, slot, place, copy)
                )
            return carry

        lax.fori_loop(0, steps, one, 0)

    def write(step, slot, place, copy):
        piece = step // 2
        first = pl.multiple_of(piece * rows, rows)
        tile = stage[slot, pl.ds(first, rows), :].astype(jnp.int32).astype(jnp.float32)
        tiles[place] = tile * factors[slot, pl.ds(piece, 1), :]
        copy.start()

    def finish(step, slot, place, copy):
        copy.wait()

    each(write)
    each(finish)


def unpack(messages, where, codes, group, depth, order, steps, before=None):
    pairs = codes.shape[1]
    slots = len(order)
    height = depth * LANES + 16
    smem = pl.BlockSpec(memory_space=pltpu.SMEM)
    operands = [where, codes, *messages] + ([] if before is None else [before])
    return pl.pallas_call(
        functools.partial(unpack_kernel, group, order, depth),
        out_shape=jax.ShapeDtypeStruct((steps, pairs, LANES, LANES), jnp.float32),
        in_specs=[smem, smem] + [pl.BlockSpec(memory_space=pl.ANY)] * (len(operands) - 2),
        out_specs=pl.BlockSpec(memory_space=pl.ANY),
        scratch_shapes=[
            pltpu.VMEM((slots, height, LANES), jnp.int16),
            pltpu.VMEM((slots, 16, LANES), jnp.float32),
            pltpu.VMEM((steps * pairs, LANES, LANES), jnp.float32),
            pltpu.SemaphoreType.DMA((slots,)),
            pltpu.SemaphoreType.DMA((steps * pairs,)),
        ],
        input_output_aliases={} if before is None else {len(operands) - 1: 0},
        compiler_params=pltpu.CompilerParams(vmem_limit_bytes=16 * 2**20),
        cost_estimate=pl.CostEstimate(
            flops=steps * pairs * LANES * LANES, bytes_accessed=steps * pairs * LANES * LANES * 3, transcendentals=0
        ),
        name="unpack",
    )(*operands)


def ring_place(chip, chips):
    return jnp.where(chip % 2 == 0, chip // 2, chips - 1 - chip // 2)


def per_device(cache, queries, plan, pair_codes):
    count = lax.axis_size("blk")
    myself = lax.axis_index("blk").astype(jnp.int32)
    local_blocks, rows, width = cache.shape
    slots = plan.shape[1]
    steps = pair_codes.shape[1]
    depth = steps // 2
    chips = count // 2
    half = chips // 2
    core = myself % 2
    place = ring_place(myself // 2, chips)
    ring = list(range(0, chips, 2)) + list(range(chips - 1, 0, -2))
    hops = jnp.arange(1, slots + 1, dtype=jnp.int32)

    def meta_of(holder):
        served = (holder - hops) % count
        lines = [plan[served, hops - 1] - holder * local_blocks]
        for t in range(depth):
            shard = (served - (served - core) % 2 - 2 * t) % count
            away = (place - ring_place(shard // 2, chips)) % chips
            pair = 2 * jnp.abs(away - half) + jnp.where(away > half, 1, 0)
            lines.append(jnp.where(away == 0, 0, jnp.where(away == half, 1, pair)))
        return jnp.stack(lines)

    def hop(x, by):
        pairs = [
            (2 * ring[p] + k, 2 * ring[(p + by) % chips] + k) for p in range(chips) for k in range(2)
        ]
        return lax.ppermute(x, "blk", pairs)

    part = rows // PARTS
    way = [1] * (PARTS // 2) + [-1] * (PARTS // 2)
    turns = [q for pair in zip(range(PARTS // 2), range(PARTS // 2, PARTS)) for q in pair]
    held = [[queries[q * part : (q + 1) * part]] for q in range(PARTS)]
    flat = cache.reshape(local_blocks * rows, width)
    sibling = lax.ppermute(flat, "blk", [(d, d ^ 1) for d in range(count)])
    sources = (flat, sibling)

    def shard_pieces(away):
        if away == 0:
            return [queries]
        return [held[q][away if way[q] > 0 else chips - away] for q in range(PARTS)]

    pairs = [(0, half)] + [(half - d, half + d) for d in range(1, half)]
    done = [[], []]
    for step in range(1, chips):
        ready = step - half - 2
        if ready >= 0:
            for other in range(2):
                q = turns[-1 - other]
                held[q][-1], done[other][ready] = lax.optimization_barrier((held[q][-1], done[other][ready]))
        for q in turns:
            held[q].append(hop(held[q][-1], way[q]))
        if half <= step < chips - 1:
            pieces = [piece for away in pairs[step - half] for piece in shard_pieces(away)]
            for other, blocks in enumerate(sources):
                done[other].append(early(blocks, pieces))
    final = [piece for away in pairs[-1] for piece in shard_pieces(away)]
    done = lax.optimization_barrier(done)

    far, near = list(range(slots - 1, slots // 2 - 1, -1)), list(range(slots // 2))
    orders = [[], []]
    for other, group in enumerate((1, 2)):
        ahead, behind = far[:], near[:]
        while ahead or behind:
            orders[other] += ahead[:group] + behind[:1]
            ahead, behind = ahead[group:], behind[1:]
        assert sorted(orders[other]) == list(range(slots))
    where = jnp.stack([myself, jnp.int32(count)])
    early_sends = slots // 2
    received, scores = [], None
    for other, blocks in enumerate(sources):
        packed = list(score(meta_of(myself ^ other), blocks, done[other], final, orders[other], depth, 12 + chips))
        if other:
            scores = unpack(received, where, pair_codes[0], 0, depth, orders[0], steps)
            packed[early_sends:], scores = lax.optimization_barrier((packed[early_sends:], scores))
        received = [
            lax.ppermute(tiles, "blk", [(d, ((d ^ other) - slot - 1) % count) for d in range(count)])
            for slot, tiles in zip(orders[other], packed)
        ]
    return unpack(received, where, pair_codes[0], 1, depth, orders[1], steps, scores)[None]


def solution(mesh):
    placed = (
        P(("groups", "blk"), None, None),
        P(("groups", "blk"), None),
        P("groups", None),
        P(("groups", "blk"), None, None),
    )
    return jax.shard_map(
        per_device,
        mesh=mesh,
        in_specs=placed,
        out_specs=P(("groups", "blk"), None, None, None, None),
        check_vma=False,
    )
```

```python
import functools

import jax
import jax.numpy as jnp
from jax import lax
from jax.experimental import pallas as pl
from jax.experimental.pallas import tpu as pltpu
from jax.sharding import PartitionSpec as P

LANES = 128
TOP = 32760.0
OCTAVE = 64.0
FLOOR = 2.0**-110
DEPTH = 2048
PARTS = 4


def pack_tile(x):
    peak = jnp.max(jnp.abs(x), axis=0, keepdims=True)
    code = jnp.ceil(jnp.log2(jnp.maximum(peak, FLOOR)) * OCTAVE)
    x = x * (jnp.exp2(code * (-1.0 / OCTAVE)) * TOP)
    x = jnp.clip(jnp.round(x), -32767.0, 32767.0)
    return x.astype(jnp.int32).astype(jnp.int16), code.astype(jnp.int32)


def multiply(cache, pieces):
    rows = jnp.concatenate([piece[...] for piece in pieces], axis=0)
    return lax.dot_general(cache[...], rows, (((1,), (1,)), ((), ())), preferred_element_type=jnp.float32)


def early_kernel(cache, *refs):
    pieces, out = refs[:-1], refs[-1]
    fresh = multiply(cache, pieces)

    @pl.when(pl.program_id(0) == 0)
    def _():
        out[...] = fresh

    @pl.when(pl.program_id(0) > 0)
    def _():
        out[...] += fresh


def piece_spec(piece):
    return pl.BlockSpec((piece.shape[0], DEPTH), lambda k: (0, k))


def early(flat, pieces):
    columns = sum(piece.shape[0] for piece in pieces)
    height, width = flat.shape
    return pl.pallas_call(
        early_kernel,
        grid=(width // DEPTH,),
        out_shape=jax.ShapeDtypeStruct((height, columns), jnp.float32),
        in_specs=[piece_spec(flat)] + [piece_spec(piece) for piece in pieces],
        out_specs=pl.BlockSpec((height, columns), lambda k: (0, 0)),
        compiler_params=pltpu.CompilerParams(
            vmem_limit_bytes=48 * 2**20, dimension_semantics=("arbitrary",)
        ),
        cost_estimate=pl.CostEstimate(
            flops=2 * flat.size * columns, bytes_accessed=2 * (height + columns) * width, transcendentals=0
        ),
        name="early",
    )(flat, *pieces)


def score_kernel(parts, count, order, depth, meta, cache, *refs):
    done, pieces, outs, total = refs[:parts], refs[parts : parts + count], refs[parts + count : -1], refs[-1]
    k = pl.program_id(0)
    rows = LANES
    each = done[0].shape[1]
    have = parts * each
    fresh = multiply(cache, pieces)

    @pl.when(k == 0)
    def _():
        for index, part in enumerate(done):
            total[:, index * each : (index + 1) * each] = part[...]
        total[:, have:] = fresh

    @pl.when(k > 0)
    def _():
        total[:, have:] += fresh

    @pl.when(k == pl.num_programs(0) - 1)
    def _():
        line = lax.broadcasted_iota(jnp.int32, (16, LANES), 0)
        for slot, out in zip(order, outs):
            first = pl.multiple_of(meta[0, slot] * rows, rows)
            scales = jnp.zeros((16, LANES), jnp.int32)
            for t in range(depth):
                column = pl.multiple_of(meta[1 + t, slot] * LANES, LANES)
                packed, code = pack_tile(total[pl.ds(first, rows), pl.ds(column, LANES)])
                out[t * rows : (t + 1) * rows, :] = packed
                scales = jnp.where(line == t, code, scales)
            out[depth * rows : depth * rows + 16, :] = scales.astype(jnp.int16)


def score(meta, flat, done, pieces, order, depth):
    slots = len(order)
    height = depth * LANES + 16
    columns = sum(piece.shape[0] for piece in pieces)
    tall, width = flat.shape
    return pl.pallas_call(
        functools.partial(score_kernel, len(done), len(pieces), order, depth),
        grid=(width // DEPTH,),
        out_shape=[jax.ShapeDtypeStruct((height, LANES), jnp.int16)] * slots,
        in_specs=[
            pl.BlockSpec(memory_space=pltpu.SMEM),
            piece_spec(flat),
        ]
        + [pl.BlockSpec(part.shape, lambda k: (0, 0)) for part in done]
        + [piece_spec(piece) for piece in pieces],
        out_specs=[pl.BlockSpec((height, LANES), lambda k: (0, 0))] * slots,
        scratch_shapes=[pltpu.VMEM((tall, sum(part.shape[1] for part in done) + columns), jnp.float32)],
        compiler_params=pltpu.CompilerParams(
            vmem_limit_bytes=48 * 2**20, dimension_semantics=("arbitrary",)
        ),
        cost_estimate=pl.CostEstimate(
            flops=2 * flat.size * columns,
            bytes_accessed=2 * (tall + columns) * width + 4 * sum(part.size for part in done) + 2 * slots * height * LANES,
            transcendentals=0,
        ),
        name="score",
    )(meta, flat, *done, *pieces)


def unpack_kernel(group, order, depth, where, codes, *refs):
    out, stage, factors, tiles, arrived, written = refs[-6:]
    steps, pairs = out.shape[:2]
    rows = LANES
    copies = [pltpu.make_async_copy(message, stage.at[slot], arrived.at[slot]) for slot, message in zip(order, refs)]
    for copy in copies:
        copy.start()
    for copy in copies:
        copy.wait()
    for slot in order:
        codes_of = stage[slot, depth * rows : depth * rows + 16, :].astype(jnp.int32).astype(jnp.float32)
        factors[slot] = jnp.exp2(codes_of * (1.0 / OCTAVE)) * (1.0 / TOP)

    def each(body):
        def one(step, carry):
            shard = where[0] + where[1] - step
            for pair in range(pairs):
                slot = codes[step, pair]
                place = step * pairs + pair
                copy = pltpu.make_async_copy(tiles.at[place], out.at[step, pair], written.at[place])
                pl.when(lax.rem(where[0] + 1 + slot + shard, 2) == group)(
                    functools.partial(body, step, slot, place, copy)
                )
            return carry

        lax.fori_loop(0, steps, one, 0)

    def write(step, slot, place, copy):
        piece = step // 2
        first = pl.multiple_of(piece * rows, rows)
        tile = stage[slot, pl.ds(first, rows), :].astype(jnp.int32).astype(jnp.float32)
        tiles[place] = tile * factors[slot, pl.ds(piece, 1), :]
        copy.start()

    def finish(step, slot, place, copy):
        copy.wait()

    each(write)
    each(finish)


def unpack(messages, where, codes, group, depth, order, steps, before=None):
    pairs = codes.shape[1]
    slots = len(order)
    height = depth * LANES + 16
    smem = pl.BlockSpec(memory_space=pltpu.SMEM)
    operands = [where, codes, *messages] + ([] if before is None else [before])
    return pl.pallas_call(
        functools.partial(unpack_kernel, group, order, depth),
        out_shape=jax.ShapeDtypeStruct((steps, pairs, LANES, LANES), jnp.float32),
        in_specs=[smem, smem] + [pl.BlockSpec(memory_space=pl.ANY)] * (len(operands) - 2),
        out_specs=pl.BlockSpec(memory_space=pl.ANY),
        scratch_shapes=[
            pltpu.VMEM((slots, height, LANES), jnp.int16),
            pltpu.VMEM((slots, 16, LANES), jnp.float32),
            pltpu.VMEM((steps * pairs, LANES, LANES), jnp.float32),
            pltpu.SemaphoreType.DMA((slots,)),
            pltpu.SemaphoreType.DMA((steps * pairs,)),
        ],
        input_output_aliases={} if before is None else {len(operands) - 1: 0},
        compiler_params=pltpu.CompilerParams(vmem_limit_bytes=16 * 2**20),
        cost_estimate=pl.CostEstimate(
            flops=steps * pairs * LANES * LANES, bytes_accessed=steps * pairs * LANES * LANES * 3, transcendentals=0
        ),
        name="unpack",
    )(*operands)


def ring_place(chip, chips):
    return jnp.where(chip % 2 == 0, chip // 2, chips - 1 - chip // 2)


def per_device(cache, queries, plan, pair_codes):
    count = lax.axis_size("blk")
    myself = lax.axis_index("blk").astype(jnp.int32)
    local_blocks, rows, width = cache.shape
    slots = plan.shape[1]
    steps = pair_codes.shape[1]
    depth = steps // 2
    chips = count // 2
    half = chips // 2
    core = myself % 2
    place = ring_place(myself // 2, chips)
    ring = list(range(0, chips, 2)) + list(range(chips - 1, 0, -2))
    hops = jnp.arange(1, slots + 1, dtype=jnp.int32)

    def meta_of(holder):
        served = (holder - hops) % count
        lines = [plan[served, hops - 1] - holder * local_blocks]
        for t in range(depth):
            shard = (served - (served - core) % 2 - 2 * t) % count
            away = (place - ring_place(shard // 2, chips)) % chips
            pair = 2 * jnp.abs(away - half) + jnp.where(away > half, 1, 0)
            lines.append(jnp.where(away == 0, 0, jnp.where(away == half, 1, pair)))
        return jnp.stack(lines)

    def hop(x, by):
        pairs = [
            (2 * ring[p] + k, 2 * ring[(p + by) % chips] + k) for p in range(chips) for k in range(2)
        ]
        return lax.ppermute(x, "blk", pairs)

    part = rows // PARTS
    way = [1] * (PARTS // 2) + [-1] * (PARTS // 2)
    turns = [q for pair in zip(range(PARTS // 2), range(PARTS // 2, PARTS)) for q in pair]
    held = [[queries[q * part : (q + 1) * part]] for q in range(PARTS)]
    flat = cache.reshape(local_blocks * rows, width)
    sibling = lax.ppermute(flat, "blk", [(d, d ^ 1) for d in range(count)])
    sources = (flat, sibling)

    def shard_pieces(away):
        if away == 0:
            return [queries]
        return [held[q][away if way[q] > 0 else chips - away] for q in range(PARTS)]

    pairs = [(0, half)] + [(half - d, half + d) for d in range(1, half)]
    done = [[], []]
    for step in range(1, chips):
        ready = step - half - 2
        if ready >= 0:
            for other in range(2):
                q = turns[-1 - other]
                held[q][-1], done[other][ready] = lax.optimization_barrier((held[q][-1], done[other][ready]))
        for q in turns:
            held[q].append(hop(held[q][-1], way[q]))
        if half <= step < chips - 1:
            pieces = [piece for away in pairs[step - half] for piece in shard_pieces(away)]
            for other, blocks in enumerate(sources):
                done[other].append(early(blocks, pieces))
    final = [piece for away in pairs[-1] for piece in shard_pieces(away)]
    done = lax.optimization_barrier(done)

    far, near = list(range(slots - 1, slots // 2 - 1, -1)), list(range(slots // 2))
    orders = [[], []]
    for other, group in enumerate((1, 2)):
        ahead, behind = far[:], near[:]
        while ahead or behind:
            orders[other] += ahead[:group] + behind[:1]
            ahead, behind = ahead[group:], behind[1:]
        assert sorted(orders[other]) == list(range(slots))
    where = jnp.stack([myself, jnp.int32(count)])
    early_sends = slots // 2
    received, scores = [], None
    for other, blocks in enumerate(sources):
        packed = list(score(meta_of(myself ^ other), blocks, done[other], final, orders[other], depth))
        if other:
            scores = unpack(received, where, pair_codes[0], 0, depth, orders[0], steps)
            packed[early_sends:], scores = lax.optimization_barrier((packed[early_sends:], scores))
        received = [
            lax.ppermute(tiles, "blk", [(d, ((d ^ other) - slot - 1) % count) for d in range(count)])
            for slot, tiles in zip(orders[other], packed)
        ]
    return unpack(received, where, pair_codes[0], 1, depth, orders[1], steps, scores)[None]


def solution(mesh):
    placed = (
        P(("groups", "blk"), None, None),
        P(("groups", "blk"), None),
        P("groups", None),
        P(("groups", "blk"), None, None),
    )
    return jax.shard_map(
        per_device,
        mesh=mesh,
        in_specs=placed,
        out_specs=P(("groups", "blk"), None, None, None, None),
        check_vma=False,
    )
```
